128 devices in a mesh: front: 8 (over x, core), grid: 16 (over y, z).
Axes of the slice: x: 4, y: 4, z: 4, core: 2. Of those that a mesh axis runs over, the one named last changes fastest.
Arguments:
- front_entries: bfloat16 [8, 9216, 4, 2048], P('front', None, None, 'grid'), may hold values from -6 to 6
- contributions: bfloat16 [20480, 128, 128], P(('front', 'grid')), may hold values from -6 to 6
- dest_owner: int32 [20480, 1], P(('front', 'grid')), may hold values from 0 to 127; in each aligned block of 160 rows (0 to 159, 160 to 319, ...) at most 2 rows name the same one
- dest_row: int32 [20480], P(('front', 'grid')), may hold values from 0 to 71
- dest_col: int32 [20480], P(('front', 'grid')), may hold values from 0 to 3
- pivot_inverse: bfloat16 [8, 1024, 1024], P('front'), may hold values from -0.1875 to 0.1875
- panel: bfloat16 [8, 8192, 1024], P('front', 'grid'), may hold values from -0.1875 to 0.1875
- pattern: int32 [8, 64, 4, 16], P('front', None, None, 'grid'), may hold values 0 or 1
- front_size: int32 [8], P('front'), may hold values from 16 to 64, as said below
Outputs:
- schur: bfloat16 [8, 8192, 4, 2048], P('front', None, None, 'grid')
The draws below stay inside these ranges and needn't reach their ends.
Inputs may be any that keep to these rules, and one draw needn't show every extreme that they name: `dest_owner`: at most 2 of one device's contribution blocks name one owner, and 2 is reached. `front_size`: some front has the full trailing size.
All inputs are finite; a program needn't handle non-finite values. No bound on the sum of `pattern` on one device may be relied on, other than what follows from the above.
Results may differ from the reference program's by a relative error of at most 0.0046.
Values may be sent and summed in bfloat16 or wider, within the bound.
A program may use at most 192 MiB of HBM per device.

```python
import math
import jax
import jax.numpy as jnp
import numpy as np
from jax import lax

BLK = 128
PIV = 1024
NBL = 4
CAP = 2
FRONTS = 8
TW = 8192
F = 9216
TWB = 64
RB = 72
CB_DEV = 160
N_GRID = 16
DEVICES = 128


def draw_front_size(key, part):
    key = jax.random.fold_in(key, 7)
    first, second = jax.random.split(key)
    sizes = jax.random.randint(first, (FRONTS,), TWB // 4, TWB + 1)
    chosen = jax.random.randint(second, (), 0, FRONTS)
    return jnp.where(jnp.arange(FRONTS) == chosen, TWB, sizes).astype(jnp.int32)


def place_ends(entries, rng, low, top_value):
    longest = entries.shape.index(max(entries.shape))
    spots = []
    for shift in (0, 1):
        where = [jax.random.randint(jax.random.fold_in(rng, axis), (), 0, length) for axis, length in enumerate(entries.shape)]
        where[longest] = (where[longest] + shift) % entries.shape[longest]
        spots.append(tuple(where))
    return entries.at[spots[0]].set(low).at[spots[1]].set(top_value)


def steps_of(own_key, dims, cuts, least, high):
    def one(dim, parts):
        heights = jax.random.uniform(jax.random.fold_in(jax.random.fold_in(own_key, 6), dim), (parts,), jnp.float32, least / len(cuts), high / len(cuts))
        return jnp.repeat(jnp.exp(heights), dims[dim] // parts).reshape((-1,) + (1,) * (len(dims) - dim - 1))

    loudness = one(*cuts[0])
    for cut in cuts[1:]:
        loudness = loudness * one(*cut)
    return loudness


def deal_out(own_key, own, number, rows, amount, top, most, lean):
    order = jax.random.permutation(own_key, amount)
    packed, ordinary = portions_of(amount, rows * top, most, lean, True), portions_of(amount, rows * top, most, lean, False)
    places = jnp.arange(amount)

    def named(tallies, rotation):
        used = int((tallies > 0).sum())
        fixed = max(1, used // 4)
        passed = fixed + (places - fixed + rotation * (used - fixed)) % max(1, amount - fixed)
        return jnp.zeros((amount,), jnp.int32).at[order[jnp.where(places < fixed, places, passed)]].set(jnp.asarray(tallies, jnp.int32))

    tallies = jnp.where(number % 4 == 0, named(packed, number // 4), named(ordinary, number - number // 4 - 1))
    mixed = jax.random.permutation(jax.random.fold_in(own, 3), amount)
    giver, taker = mixed[0:amount // 2 * 2:2], mixed[1:amount // 2 * 2:2]
    room = jnp.minimum(tallies[giver] - 1, most - tallies[taker]) // 2
    room = jnp.where((giver == order[0]) | (taker == order[0]) | (tallies[taker] == 0), 0, jnp.maximum(room, 0))
    passed = jax.random.randint(jax.random.fold_in(own, 4), (amount // 2,), 0, 1 << 20) % (room + 1)
    tallies = tallies.at[giver].add(-passed).at[taker].add(passed)
    labels = jnp.searchsorted(jnp.cumsum(tallies), jnp.arange(rows * top), side="right").astype(jnp.int32)
    grid = labels.reshape(top, rows).T
    grid = grid[jax.random.permutation(jax.random.fold_in(own, 1), rows)]
    rotation = jax.random.randint(jax.random.fold_in(own, 2), (rows, 1), 0, top)
    return jnp.take_along_axis(grid, (jnp.arange(top)[None, :] + rotation) % top, axis=1)


def portions_of(number_of, total, limit, slope, full):
    portions = [(1 << 20) // math.isqrt(grade ** slope) + 1 for grade in range(1, number_of + 1)]
    largest = limit if full else min(limit, max(-(-total // number_of), total * portions[0] // sum(portions)))
    least = 1 if total - largest >= number_of - 1 else 0
    holding, surplus = [largest] + [least] * (number_of - 1), total - largest - least * (number_of - 1)
    while surplus > 0:
        free = [i for i in range(1, number_of) if holding[i] < largest] or [i for i in range(1, number_of) if holding[i] < limit]
        pool, budget = sum([portions[i] for i in free]), surplus
        for i in free:
            more = min(limit - holding[i], max(1, budget * portions[i] // pool), surplus)
            holding[i] = holding[i] + more
            surplus = surplus - more
    return np.array(holding)


def bell_draw(stream_key, extent, deviation, most, cuts=(), held_as=jnp.bfloat16):
    array = jax.random.normal(stream_key, extent, jnp.float32) * deviation
    if len(cuts) > 0:
        array = steps_of(stream_key, extent, cuts, -0.22, 0.18) * array
    return jnp.clip(array, min=-most, max=most).astype(held_as)


def setup_inputs(seed: int = 0) -> dict:
    key_list = jax.random.split(jax.random.key(seed), 10)
    front_entries = bell_draw(key_list[0], (FRONTS, F, NBL, N_GRID * BLK), 1.0, 6.0, ((0, 8), (3, 16)))
    contributions = bell_draw(key_list[1], (DEVICES * CB_DEV, BLK, BLK), 1.0, 6.0, ((0, 128),))
    dest_owner_keys = jax.random.split(jax.random.fold_in(key_list[2], 1), (DEVICES * CB_DEV) // CB_DEV)
    dest_owner_turns = jax.random.permutation(jax.random.fold_in(key_list[2], 3), (DEVICES * CB_DEV) // CB_DEV)
    dest_owner = jax.vmap(lambda own, number: deal_out(jax.random.fold_in(key_list[2], 2), own, number, CB_DEV, DEVICES, 1, CAP, 2))(dest_owner_keys, dest_owner_turns).reshape((DEVICES * CB_DEV, 1))
    dest_row = place_ends(jax.random.randint(key_list[3], (DEVICES * CB_DEV,), 0, RB), jax.random.fold_in(key_list[3], 1), 0, RB - 1).astype(jnp.int32)
    dest_col = place_ends(jax.random.randint(key_list[4], (DEVICES * CB_DEV,), 0, NBL), jax.random.fold_in(key_list[4], 1), 0, NBL - 1).astype(jnp.int32)
    pivot_inverse = bell_draw(key_list[5], (FRONTS, PIV, PIV), PIV ** -0.5, 0.1875, ((0, 8),))
    panel = bell_draw(key_list[6], (FRONTS, TW, PIV), PIV ** -0.5, 0.1875, ((0, 8), (1, 16)))
    pattern = place_ends((jax.random.randint(key_list[7], (FRONTS, TWB, NBL, N_GRID), 0, 2) < 1).astype(jnp.int32), jax.random.fold_in(key_list[7], 1), 0, 1)
    front_size = draw_front_size(jax.random.fold_in(key_list[9], 71), 0)
    return {"front_entries": front_entries, "contributions": contributions, "dest_owner": dest_owner, "dest_row": dest_row, "dest_col": dest_col, "pivot_inverse": pivot_inverse, "panel": panel, "pattern": pattern, "front_size": front_size}


def reference(front_entries, contributions, dest_owner, dest_row, dest_col, pivot_inverse, panel, pattern, front_size):
    owner = dest_owner[:, 0]
    group = owner // N_GRID
    column = owner % N_GRID
    data = contributions.astype(jnp.float32)

    def one_front(index):
        rows = jnp.where(group == index, dest_row, RB).astype(jnp.int32)
        store = front_entries[index].astype(jnp.float32).reshape(RB, BLK, NBL, N_GRID, BLK)
        store = store.at[rows, :, dest_col, column, :].add(data, mode="drop")
        assembled = store.reshape(F, TW).astype(jnp.bfloat16)
        factor = jnp.dot(pivot_inverse[index], assembled[:PIV], preferred_element_type=jnp.float32).astype(jnp.bfloat16)
        update = jnp.dot(panel[index], factor, preferred_element_type=jnp.float32)
        blocks = pattern[index].reshape(TWB, TWB).astype(jnp.float32)
        spread = jnp.broadcast_to(blocks[:, None, :, None], (TWB, BLK, TWB, BLK)).reshape(TW, TW)
        inside = (jnp.arange(TW) // BLK) < front_size[index]
        lower = assembled[PIV:].astype(jnp.float32)
        result = jnp.where(inside[:, None] & inside[None, :], lower - spread * update, 0.0)
        return result.astype(jnp.bfloat16).reshape(TW, NBL, N_GRID * BLK)

    return lax.map(one_front, jnp.arange(FRONTS))
```

```python
import functools

import jax
import jax.numpy as jnp
from jax import lax
from jax.experimental import pallas as pl
from jax.experimental.pallas import tpu as pltpu
from jax.sharding import PartitionSpec as P

BLK = 128
PIV = 1024
NBL = 4
CAP = 2
MESH = pl.DeviceIdType.MESH
PARTS = ((0, 96), (96, 80), (176, 80))
ORDERS = ((0, 1, 2), (1, 2, 0), (2, 0, 1))


def at_axis(axis, where, rows=None):
    index = [slice(None)] * 5
    index[axis] = where
    if rows is not None:
        index[3] = pl.ds(rows[0], rows[1])
    return tuple(index)


def exchange_kernel(
    table, blocks, meta, panel,
    arrived, meta_out, panel_full,
    slots, a1, a2, b1, b2, c1, c2, m1, m2,
    send_sem, recv_sem, own_sem, gsend_sem, grecv_sem, gown_sem,
):
    f = lax.axis_index("front")
    g = lax.axis_index("grid")
    y, z = g // 4, g % 4
    me = (f, y, z)

    def device(axis, coordinate):
        if axis == 0:
            return (coordinate, g)
        if axis == 1:
            return (f, coordinate * 4 + z)
        return (f, y * 4 + coordinate)

    def peer(axis, d):
        if axis == 0:
            return ((f // 2 + d // 2) % 4) * 2 + (f + d) % 2
        return (me[axis] + d) % 4

    offsets = ((2, 6, 4, 3, 7, 5, 1), (1, 3, 2), (1, 3, 2))

    barrier = pltpu.get_barrier_semaphore()
    for axis in range(3):
        for d in offsets[axis]:
            pl.semaphore_signal(
                barrier, inc=1, device_id=device(axis, peer(axis, d)), device_id_type=MESH
            )

    gown = pltpu.make_async_copy(panel, panel_full.at[y, z], gown_sem)
    gown.start()

    def fill(d, carry):
        for j in range(CAP):
            slots[d // 16, (d // 4) % 4, d % 4, pl.ds(j * BLK, BLK), :] = blocks[table[d * CAP + j]]
        return carry

    lax.fori_loop(0, 128, fill, 0)
    pl.semaphore_wait(barrier, 13)

    chains = []
    for part, (rows, order) in enumerate(zip(PARTS, ORDERS)):
        s1, s2 = ((a1, a2), (b1, b2), (c1, c2))[part]
        chains.append(((slots, rows), (s1, None), (s2, None), (arrived, rows), order))
    chains.append(((meta, None), (m1, None), (m2, None), (meta_out, None), (0, 1, 2)))

    def view(buffer, axis, where):
        ref, rows = buffer
        return ref.at[at_axis(axis, where, rows)]

    pending = []

    def start(part, stage):
        chain = chains[part]
        source, target, axis = chain[stage], chain[stage + 1], chain[4][stage]
        own = pltpu.make_async_copy(
            view(source, axis, me[axis]), view(target, axis, me[axis]), own_sem.at[part, stage]
        )
        own.start()
        for d in offsets[axis]:
            there = peer(axis, d)
            pltpu.make_async_remote_copy(
                src_ref=view(source, axis, there),
                dst_ref=view(target, axis, me[axis]),
                send_sem=send_sem.at[part, stage],
                recv_sem=recv_sem.at[part, stage],
                device_id=device(axis, there),
                device_id_type=MESH,
            ).start()
        count = len(offsets[axis])
        whole = pltpu.make_async_remote_copy(
            src_ref=view(source, axis, pl.ds(0, count)),
            dst_ref=view(target, axis, pl.ds(0, count)),
            send_sem=send_sem.at[part, stage],
            recv_sem=recv_sem.at[part, stage],
            device_id=device(axis, peer(axis, 1)),
            device_id_type=MESH,
        )
        pending.append(whole)
        return own, whole

    def finish(handles):
        own, whole = handles
        own.wait()
        whole.wait_recv()

    gathers = []

    def place(half, dp, ds):
        if half == 0:
            return (y + dp + 4) % 4, (z + ds + 4) % 4
        return (y + ds + 4) % 4, (z + dp + 4) % 4

    def give(half, dp, ds, piece, along, step):
        py, pz = place(half, dp, ds)
        first, count = half * 256, 256
        if piece is not None:
            first, count = first + 128 * piece, 128
        rows = pl.ds(first, count)
        axis = (1, 2)[half] if along == 0 else (2, 1)[half]
        if (dp, ds) == (0, 0):
            source = panel.at[rows]
        else:
            source = panel_full.at[py, pz, rows]
        index = len(gathers)
        copy = pltpu.make_async_remote_copy(
            src_ref=source,
            dst_ref=panel_full.at[py, pz, rows],
            send_sem=gsend_sem.at[index],
            recv_sem=grecv_sem.at[index],
            device_id=device(axis, peer(axis, step % 4)),
            device_id_type=MESH,
        )
        copy.start()
        gathers.append(copy)
        return copy

    got = {}

    def gather_0():
        for half in (0, 1):
            for step in (1, -1):
                got[half, "p", step] = give(half, 0, 0, None, 0, step)
        for half in (0, 1):
            for step in (1, -1):
                got[half, "s", 0, step] = give(half, 0, 0, None, 1, step)

    def gather_1():
        for half in (0, 1):
            for step in (1, -1):
                got[half, "p", step].wait_recv()
        for half in (0, 1):
            for step, piece in ((1, 0), (-1, 1)):
                got[half, "pf", step] = give(half, -step, 0, piece, 0, step)
        for half in (0, 1):
            for dp in (-1, 1):
                for step in (1, -1):
                    got[half, "s", dp, step] = give(half, dp, 0, None, 1, step)
        forward(0)

    def forward(dp):
        for half in (0, 1):
            for step, piece in ((1, 0), (-1, 1)):
                got[half, "s", dp, step].wait_recv()
                got[half, "sf", dp, step] = give(half, dp, -step, piece, 1, step)

    def gather_2():
        for half in (0, 1):
            for step in (1, -1):
                got[half, "pf", step].wait_recv()
        for half in (0, 1):
            for step in (1, -1):
                got[half, "s", 2, step] = give(half, 2, 0, None, 1, step)
        forward(-1)
        forward(1)

    def gather_3():
        forward(2)

    first = [start(part, 0) for part in (3, 0, 1, 2)]
    gather_0()
    for handles in first:
        finish(handles)
    second = [start(part, 1) for part in (3, 0, 1, 2)]
    gather_1()
    for handles in second:
        finish(handles)
    third = [start(part, 2) for part in (3, 0, 1, 2)]
    gather_2()
    for handles in third:
        finish(handles)
    gather_3()
    for dp in (0, -1, 1, 2):
        for half in (0, 1):
            for step in (1, -1):
                got[half, "sf", dp, step].wait_recv()
    gown.wait()
    for whole in pending:
        whole.wait_send()
    for copy in gathers:
        copy.wait_send()


def exchange(table, blocks, meta, panel):
    def stage(rows):
        return pltpu.VMEM((8, 4, 4, rows, BLK), jnp.bfloat16)

    any_space = pl.BlockSpec(memory_space=pl.ANY)
    sizes = [rows for _, rows in PARTS]
    return pl.pallas_call(
        exchange_kernel,
        out_shape=(
            jax.ShapeDtypeStruct((8, 4, 4, CAP * BLK, BLK), jnp.bfloat16),
            jax.ShapeDtypeStruct((8, 4, 4, 1, BLK), jnp.int32),
            jax.ShapeDtypeStruct((4, 4) + panel.shape, jnp.bfloat16),
        ),
        in_specs=[
            pl.BlockSpec(memory_space=pltpu.SMEM),
            pl.BlockSpec(memory_space=pltpu.VMEM),
            any_space,
            any_space,
        ],
        out_specs=(any_space, any_space, any_space),
        scratch_shapes=[
            stage(CAP * BLK),
            stage(sizes[0]), stage(sizes[0]),
            stage(sizes[1]), stage(sizes[1]),
            stage(sizes[2]), stage(sizes[2]),
            pltpu.VMEM((8, 4, 4, 1, BLK), jnp.int32),
            pltpu.VMEM((8, 4, 4, 1, BLK), jnp.int32),
            pltpu.SemaphoreType.DMA((4, 3)),
            pltpu.SemaphoreType.DMA((4, 3)),
            pltpu.SemaphoreType.DMA((4, 3)),
            pltpu.SemaphoreType.DMA((40,)),
            pltpu.SemaphoreType.DMA((40,)),
            pltpu.SemaphoreType.DMA,
        ],
        compiler_params=pltpu.CompilerParams(
            collective_id=0, has_side_effects=True, vmem_limit_bytes=50 * 2**20
        ),
        name="exchange",
    )(table, blocks, meta, panel)


CHUNK = 512
NF = 9


def front_kernel(
    places, pattern, size, front, arrived, pivot, panel, out,
    acc, front_v, arrived_v, pivot_v, panel_v, out_v, top, factor, update,
    front_sem, arrived_sem, pivot_sem, panel_sem, out_sem,
):
    column = lax.axis_index("grid")
    limit = size[0]
    rows = front.shape[0] // NF
    chunks = panel.shape[0]
    slots = arrived.shape[0]

    def front_copy(i):
        part = pl.ds(i * rows, rows)
        return pltpu.make_async_copy(front.at[part], front_v.at[part], front_sem.at[i])

    def arrived_copy(i):
        part = pl.ds(i * (slots // 4), slots // 4)
        return pltpu.make_async_copy(arrived.at[part], arrived_v.at[part], arrived_sem.at[i])

    def panel_copy(c, slot):
        return pltpu.make_async_copy(panel.at[c], panel_v.at[slot], panel_sem.at[slot])

    def out_copy(c, slot):
        return pltpu.make_async_copy(
            out_v.at[slot], out.at[pl.ds(c * CHUNK * NBL, CHUNK * NBL)], out_sem.at[slot]
        )

    pivot_copy = pltpu.make_async_copy(pivot, pivot_v, pivot_sem)
    for i in range(NF):
        front_copy(i).start()
    for i in range(4):
        arrived_copy(i).start()
    pivot_copy.start()
    panel_copy(0, 0).start()
    panel_copy(1, 1).start()

    for i in range(NF):
        front_copy(i).wait()

        def widen(j, carry):
            part = pl.ds(i * rows + j * 512, 512)
            acc[part, :] = front_v[part, :].astype(jnp.float32)
            return carry

        lax.fori_loop(0, rows // 512, widen, 0)

    for i in range(4):
        arrived_copy(i).wait()

        def add(j, carry):
            slot = i * (slots // 4) + j
            place = places[slot]

            @pl.when(place < acc.shape[0] // BLK)
            def _():
                start = (place // NBL) * (BLK * NBL) + place % NBL
                part = pl.ds(start, BLK, stride=NBL)
                acc[part, :] += arrived_v[slot].astype(jnp.float32)

            return carry

        lax.fori_loop(0, slots // 4, add, 0)

    for k in range(NBL):
        for i in range(PIV // 256):
            part = pl.ds(i * 256 * NBL + k, 256, stride=NBL)
            top[pl.ds(i * 256, 256), pl.ds(k * BLK, BLK)] = acc[part, :].astype(jnp.bfloat16)
    pivot_copy.wait()
    factor[...] = jnp.dot(pivot_v[...], top[...], preferred_element_type=jnp.float32).astype(
        jnp.bfloat16
    )

    def step(c, carry):
        slot = c % 2
        panel_copy(c, slot).wait()

        @pl.when(c >= 2)
        def _():
            out_copy(c - 2, slot).wait()

        update[...] = jnp.dot(panel_v[slot], factor[...], preferred_element_type=jnp.float32)

        @pl.when(c + 2 < chunks)
        def _():
            panel_copy(c + 2, slot).start()

        for i in range(CHUNK // BLK):
            row = c * (CHUNK // BLK) + i
            for k in range(NBL):
                keep = jnp.logical_and(row < limit, k * 16 + column < limit)
                chosen = pattern[row, k].astype(jnp.float32)
                part = pl.ds((PIV + row * BLK) * NBL + k, BLK, stride=NBL)
                lower = acc[part, :].astype(jnp.bfloat16).astype(jnp.float32)
                taken = update[pl.ds(i * BLK, BLK), pl.ds(k * BLK, BLK)]
                acc[part, :] = jnp.where(keep, lower - chosen * taken, 0.0)
            here = pl.ds((PIV + row * BLK) * NBL, BLK * NBL)
            out_v[slot, pl.ds(i * BLK * NBL, BLK * NBL), :] = acc[here, :].astype(jnp.bfloat16)
        out_copy(c, slot).start()
        return carry

    lax.fori_loop(0, chunks, step, 0)
    out_copy(chunks - 2, 0).wait()
    out_copy(chunks - 1, 1).wait()


def schur_of_front(places, pattern, size, front, arrived, pivot, panel):
    any_space = pl.BlockSpec(memory_space=pl.ANY)
    smem = pl.BlockSpec(memory_space=pltpu.SMEM)
    trail = panel.shape[0] * panel.shape[1]
    return pl.pallas_call(
        front_kernel,
        out_shape=jax.ShapeDtypeStruct((trail * NBL, BLK), jnp.bfloat16),
        in_specs=[smem, smem, smem, any_space, any_space, any_space, any_space],
        out_specs=any_space,
        scratch_shapes=[
            pltpu.VMEM(front.shape, jnp.float32),
            pltpu.VMEM(front.shape, jnp.bfloat16),
            pltpu.VMEM(arrived.shape, jnp.bfloat16),
            pltpu.VMEM(pivot.shape, jnp.bfloat16),
            pltpu.VMEM((2,) + panel.shape[1:], jnp.bfloat16),
            pltpu.VMEM((2, CHUNK * NBL, BLK), jnp.bfloat16),
            pltpu.VMEM((PIV, NBL * BLK), jnp.bfloat16),
            pltpu.VMEM((PIV, NBL * BLK), jnp.bfloat16),
            pltpu.VMEM((CHUNK, NBL * BLK), jnp.float32),
            pltpu.SemaphoreType.DMA((NF,)),
            pltpu.SemaphoreType.DMA((4,)),
            pltpu.SemaphoreType.DMA,
            pltpu.SemaphoreType.DMA((2,)),
            pltpu.SemaphoreType.DMA((2,)),
        ],
        compiler_params=pltpu.CompilerParams(vmem_limit_bytes=58 * 2**20),
        name="front",
    )(places, pattern, size, front, arrived, pivot, panel)


def per_device(
    front_entries,
    contributions,
    dest_owner,
    dest_row,
    dest_col,
    pivot_inverse,
    panel,
    pattern,
    front_size,
):
    devices = lax.axis_size("front") * lax.axis_size("grid")
    count = contributions.shape[0]
    total_rows = front_entries.shape[1]
    sentinel = total_rows // BLK * NBL
    owner = dest_owner[:, 0]
    position = jnp.arange(count, dtype=jnp.int32)
    same_owner = owner[:, None] == owner[None, :]
    before = position[None, :] < position[:, None]
    ranking = jnp.sum((same_owner & before).astype(jnp.int32), axis=1)
    slots = owner * CAP + ranking
    table = jnp.zeros((devices * CAP,), jnp.int32).at[slots].set(position)
    targets = (
        jnp.full((devices * CAP,), sentinel, jnp.int32).at[slots].set(dest_row * NBL + dest_col)
    )
    meta = jnp.pad(targets.reshape(8, 4, 4, 1, CAP), ((0, 0),) * 4 + ((0, BLK - CAP),))
    arrived, meta, whole_panel = exchange(table, contributions, meta, panel[0])
    places = meta[..., 0, :CAP].reshape(devices * CAP)
    out = schur_of_front(
        places,
        pattern[0, :, :, 0],
        front_size,
        front_entries.reshape(total_rows * NBL, BLK),
        arrived.reshape(devices * CAP, BLK, BLK),
        pivot_inverse[0],
        whole_panel.reshape(16, panel.shape[1], panel.shape[2]),
    )
    return out.reshape(1, -1, NBL, BLK)


def solution(mesh):
    placed = (
        P("front", None, None, "grid"),
        P(("front", "grid"), None, None),
        P(("front", "grid"), None),
        P(("front", "grid")),
        P(("front", "grid")),
        P("front", None, None),
        P("front", "grid", None),
        P("front", None, None, "grid"),
        P("front"),
    )
    return jax.shard_map(
        per_device,
        mesh=mesh,
        in_specs=placed,
        out_specs=P("front", None, None, "grid"),
        check_vma=False,
    )
```

```python
import functools

import jax
import jax.numpy as jnp
from jax import lax
from jax.experimental import pallas as pl
from jax.experimental.pallas import tpu as pltpu
from jax.sharding import PartitionSpec as P

BLK = 128
PIV = 1024
NBL = 4
CAP = 2
MESH = pl.DeviceIdType.MESH
PARTS = ((0, 96), (96, 80), (176, 80))
ORDERS = ((0, 1, 2), (1, 2, 0), (2, 0, 1))


def at_axis(axis, where, rows=None):
    index = [slice(None)] * 5
    index[axis] = where
    if rows is not None:
        index[3] = pl.ds(rows[0], rows[1])
    return tuple(index)


def front_kernel(
    table, size, pattern, blocks, meta, front, pivot, panel,
    out, arrived, panel_full, a1, a2, b1, b2, c1, c2,
    slots, blocks_v, sums, lower, top_front, pivot_v, top, factor, panel_v, update, out_v, wide,
    m1, m2, m3, places, chain_v, chain,
    send_sem, recv_sem, own_sem, gsend_sem, grecv_sem, gown_sem,
    load_sem, arrived_sem, chain_sem, panel_sem, out_sem,
):
    f = lax.axis_index("front")
    g = lax.axis_index("grid")
    y, z = g // 4, g % 4
    me = (f, y, z)

    def device(axis, coordinate):
        if axis == 0:
            return (coordinate, g)
        if axis == 1:
            return (f, coordinate * 4 + z)
        return (f, y * 4 + coordinate)

    def peer(axis, d):
        if axis == 0:
            return ((f // 2 + d // 2) % 4) * 2 + (f + d) % 2
        return (me[axis] + d) % 4

    offsets = ((2, 6, 4, 3, 7, 5, 1), (1, 3, 2), (1, 3, 2))

    barrier = pltpu.get_barrier_semaphore()
    for axis in range(3):
        for d in offsets[axis]:
            pl.semaphore_signal(
                barrier, inc=1, device_id=device(axis, peer(axis, d)), device_id_type=MESH
            )

    top_rows = PIV * NBL
    load_blocks = pltpu.make_async_copy(blocks, blocks_v, load_sem.at[0])
    load_top = pltpu.make_async_copy(front.at[pl.ds(0, top_rows)], top_front, load_sem.at[1])
    load_lower = pltpu.make_async_copy(
        front.at[pl.ds(top_rows, lower.shape[0])], lower, load_sem.at[2]
    )
    load_pivot = pltpu.make_async_copy(pivot, pivot_v, load_sem.at[3])
    gown = pltpu.make_async_copy(panel, panel_full.at[y, z], gown_sem)
    load_blocks.start()
    gown.start()
    load_blocks.wait()

    def fill(d, carry):
        for j in range(CAP):
            slots[d // 16, (d // 4) % 4, d % 4, pl.ds(j * BLK, BLK), :] = blocks_v[
                table[d * CAP + j]
            ]
        return carry

    lax.fori_loop(0, 128, fill, 0)
    pl.semaphore_wait(barrier, 13)

    chains = []
    for part, (rows, order) in enumerate(zip(PARTS, ORDERS)):
        s1, s2 = ((a1, a2), (b1, b2), (c1, c2))[part]
        chains.append(((slots, rows), (s1, None), (s2, None), (arrived, rows), order))
    chains.append(((meta, None), (m1, None), (m2, None), (m3, None), (0, 1, 2)))

    def view(buffer, axis, where):
        ref, rows = buffer
        return ref.at[at_axis(axis, where, rows)]

    pending = {}

    def start(part, stage):
        steps = chains[part]
        source, target, axis = steps[stage], steps[stage + 1], steps[4][stage]
        own = pltpu.make_async_copy(
            view(source, axis, me[axis]), view(target, axis, me[axis]), own_sem.at[part, stage]
        )
        own.start()
        for d in offsets[axis]:
            there = peer(axis, d)
            pltpu.make_async_remote_copy(
                src_ref=view(source, axis, there),
                dst_ref=view(target, axis, me[axis]),
                send_sem=send_sem.at[part, stage],
                recv_sem=recv_sem.at[part, stage],
                device_id=device(axis, there),
                device_id_type=MESH,
            ).start()
        count = len(offsets[axis])
        whole = pltpu.make_async_remote_copy(
            src_ref=view(source, axis, pl.ds(0, count)),
            dst_ref=view(target, axis, pl.ds(0, count)),
            send_sem=send_sem.at[part, stage],
            recv_sem=recv_sem.at[part, stage],
            device_id=device(axis, peer(axis, 1)),
            device_id_type=MESH,
        )
        pending[part, stage] = (own, whole)

    def finish(part, stage):
        own, whole = pending[part, stage]
        own.wait()
        whole.wait_recv()

    gathers = []
    got = {}

    def place(half, dp, ds):
        if half == 0:
            return (y + dp + 4) % 4, (z + ds + 4) % 4
        return (y + ds + 4) % 4, (z + dp + 4) % 4

    def give(key, half, dp, ds, piece, along, step):
        py, pz = place(half, dp, ds)
        first, count = half * 256, 256
        if piece is not None:
            first, count = first + 128 * piece, 128
        rows = pl.ds(first, count)
        axis = (1, 2)[half] if along == 0 else (2, 1)[half]
        source = panel.at[rows] if (dp, ds) == (0, 0) else panel_full.at[py, pz, rows]
        index = len(gathers)
        copy = pltpu.make_async_remote_copy(
            src_ref=source,
            dst_ref=panel_full.at[py, pz, rows],
            send_sem=gsend_sem.at[index],
            recv_sem=grecv_sem.at[index],
            device_id=device(axis, peer(axis, step % 4)),
            device_id_type=MESH,
        )
        copy.start()
        gathers.append(copy)
        got[key] = copy

    def each(act):
        for half in (0, 1):
            for step, piece in ((1, 0), (-1, 1)):
                act(half, step, piece)

    def first_line():
        each(lambda h, s, p: give((h, "p", s), h, 0, 0, None, 0, s))

    def second_line(dp):
        each(lambda h, s, p: give((h, "s", dp, s), h, dp, 0, None, 1, s))

    def first_forward():
        each(lambda h, s, p: got[h, "p", s].wait_recv())
        each(lambda h, s, p: give((h, "pf", s), h, -s, 0, p, 0, s))

    def second_forward(dp):
        each(lambda h, s, p: got[h, "s", dp, s].wait_recv())
        each(lambda h, s, p: give((h, "sf", dp, s), h, dp, -s, p, 1, s))

    def landed(kind, *rest):
        each(lambda h, s, p: got[(h, kind) + rest + (s,)].wait_recv())

    def make_tables():
        def spread(d, carry):
            places[pl.ds(d * CAP, CAP), :] = m3[d // 16, (d // 4) % 4, d % 4]
            return carry

        lax.fori_loop(0, 128, spread, 0)
        where = places[...]
        slot = lax.broadcasted_iota(jnp.int32, where.shape, 0)
        lane = lax.broadcasted_iota(jnp.int32, where.shape, 1)
        for half in range(2):
            mine = lane + half * BLK
            along = jnp.sum(jnp.where(slot == mine, where, 0), axis=0, keepdims=True)
            same = jnp.logical_and(where == along, slot < mine)
            chain_v[half : half + 1, :] = jnp.max(
                jnp.where(same, slot, -1), axis=0, keepdims=True
            )
        for third in range(3):
            same = where == lane + third * BLK
            chain_v[2 + third : 3 + third, :] = jnp.max(
                jnp.where(same, slot, -1), axis=0, keepdims=True
            )
        copy = pltpu.make_async_copy(chain_v, chain, chain_sem)
        copy.start()
        copy.wait()

    def block_of(t):
        d = t // CAP
        return slots[d // 16, (d // 4) % 4, d % 4, pl.ds((t % CAP) * BLK, BLK), :].astype(
            jnp.float32
        )

    def add_up():
        sums[0] = block_of(0)

        def one(t, carry):
            before = chain[t // BLK, t % BLK]
            so_far = sums[jnp.maximum(before, 0)]
            sums[t] = block_of(t) + jnp.where(before >= 0, so_far, 0.0)
            return carry

        lax.fori_loop(1, sums.shape[0], one, 0)

    def assembled(source, row, block_row):
        here = pl.ds(row * BLK * NBL, BLK * NBL)
        wide[...] = source[here, :].astype(jnp.float32)
        values = []
        for k in range(NBL):
            p = block_row * NBL + k
            last = chain[2 + p // BLK, p % BLK]
            total = sums[jnp.maximum(last, 0)]
            part = pl.ds(k, BLK, stride=NBL)
            value = wide[part, :] + jnp.where(last >= 0, total, 0.0)
            wide[part, :] = value
            values.append(value)
        return here, values

    def make_factor():
        def one(row, carry):
            _, values = assembled(top_front, row, row)
            for k in range(NBL):
                top[pl.ds(row * BLK, BLK), pl.ds(k * BLK, BLK)] = values[k].astype(jnp.bfloat16)
            return carry

        lax.fori_loop(0, PIV // BLK, one, 0)
        load_pivot.wait()
        factor[...] = jnp.dot(
            pivot_v[...], top[...], preferred_element_type=jnp.float32
        ).astype(jnp.bfloat16)

    def make_lower():
        def one(row, carry):
            here, _ = assembled(lower, row, row + PIV // BLK)
            lower[here, :] = wide[...].astype(jnp.bfloat16)
            return carry

        lax.fori_loop(0, lower.shape[0] // (BLK * NBL), one, 0)

    limit = size[0]

    def updates(count, decode):
        def load(i):
            half, py, pz = decode(i)
            return pltpu.make_async_copy(
                panel_full.at[py, pz, pl.ds(half * 256, 256)], panel_v.at[i % 2], panel_sem.at[i % 2]
            )

        def store(i):
            half, py, pz = decode(i)
            first = ((py * 4 + pz) * 512 + half * 256) * NBL
            return pltpu.make_async_copy(
                out_v.at[i % 2], out.at[pl.ds(first, 256 * NBL)], out_sem.at[i % 2]
            )

        load(0).start()

        def one(i, carry):
            load(i).wait()

            @pl.when(i + 1 < count)
            def _():
                load(i + 1).start()

            @pl.when(i >= 2)
            def _():
                store(i - 2).wait()

            update[...] = jnp.dot(
                panel_v[i % 2], factor[...], preferred_element_type=jnp.float32
            )
            half, py, pz = decode(i)
            for j in range(2):
                row = (py * 4 + pz) * 4 + half * 2 + j
                wide[...] = lower[pl.ds(row * BLK * NBL, BLK * NBL), :].astype(jnp.float32)
                for k in range(NBL):
                    keep = jnp.logical_and(row < limit, k * 16 + g < limit)
                    chosen = pattern[row, k].astype(jnp.float32)
                    part = pl.ds(k, BLK, stride=NBL)
                    taken = update[pl.ds(j * BLK, BLK), pl.ds(k * BLK, BLK)]
                    wide[part, :] = jnp.where(keep, wide[part, :] - chosen * taken, 0.0)
                out_v[i % 2, pl.ds(j * BLK * NBL, BLK * NBL), :] = wide[...].astype(jnp.bfloat16)
            store(i).start()
            return carry

        lax.fori_loop(0, count, one, 0)
        for i in (count - 2, count - 1):
            store(i).wait()

    def near(i):
        half, a, b = i % 2, (i // 2) % 3, i // 6
        dp, ds = a + a // 2, b + b // 2
        return spot(half, dp, ds)

    def spot(half, dp, ds):
        return half, (y + dp * (1 - half) + ds * half) % 4, (z + dp * half + ds * (1 - half)) % 4

    def far(i):
        half, a, b = i % 2, (i // 2) % 3, i // 6
        d = a + a // 2
        return spot(half, d * (1 - b) + 2 * b, d * b + 2 * (1 - b))

    def last(i):
        return spot(i, 2, 2)

    start(3, 0)
    for part in range(3):
        start(part, 0)
    first_line()
    second_line(0)
    load_top.start()
    load_lower.start()
    load_pivot.start()
    finish(3, 0)
    start(3, 1)
    for part in range(3):
        finish(part, 0)
        start(part, 1)
    finish(3, 1)
    start(3, 2)
    first_forward()
    second_forward(0)
    for part in range(3):
        finish(part, 1)
        start(part, 2)
    second_line(-1)
    finish(3, 2)
    make_tables()
    for part in range(3):
        pending[part, 0][1].wait_send()
    for part in range(3):
        finish(part, 2)
    second_line(1)
    landed("pf")
    second_line(2)
    back = pltpu.make_async_copy(arrived, slots, arrived_sem)
    back.start()
    second_forward(-1)
    back.wait()
    add_up()
    second_forward(1)
    load_top.wait()
    make_factor()
    load_lower.wait()
    make_lower()
    second_forward(2)
    gown.wait()
    updates(18, near)
    for dp in (0, -1, 1):
        landed("sf", dp)
    updates(12, far)
    landed("sf", 2)
    updates(2, last)
    for (part, stage), (_, whole) in pending.items():
        if part == 3 or stage > 0:
            whole.wait_send()
    for copy in gathers:
        copy.wait_send()


def schur_of_front(table, size, pattern, blocks, meta, front, pivot, panel):
    grid_of = (8, 4, 4)
    any_space = pl.BlockSpec(memory_space=pl.ANY)
    smem = pl.BlockSpec(memory_space=pltpu.SMEM)
    sizes = [rows for _, rows in PARTS for _ in range(2)]
    trail = front.shape[0] - PIV * NBL
    dma = pltpu.SemaphoreType.DMA
    outs = [
        (trail, BLK),
        grid_of + (CAP * BLK, BLK),
        (4, 4) + panel.shape,
    ] + [grid_of + (rows, BLK) for rows in sizes]
    small = pltpu.VMEM(grid_of + (CAP, BLK), jnp.int32)
    return pl.pallas_call(
        front_kernel,
        out_shape=[jax.ShapeDtypeStruct(shape, jnp.bfloat16) for shape in outs],
        in_specs=[smem, smem, smem, any_space, any_space, any_space, any_space, any_space],
        out_specs=[any_space] * len(outs),
        scratch_shapes=[
            pltpu.VMEM(grid_of + (CAP * BLK, BLK), jnp.bfloat16),
            pltpu.VMEM(blocks.shape, jnp.bfloat16),
            pltpu.VMEM((128 * CAP, BLK, BLK), jnp.float32),
            pltpu.VMEM((trail, BLK), jnp.bfloat16),
            pltpu.VMEM((PIV * NBL, BLK), jnp.bfloat16),
            pltpu.VMEM(pivot.shape, jnp.bfloat16),
            pltpu.VMEM((PIV, NBL * BLK), jnp.bfloat16),
            pltpu.VMEM((PIV, NBL * BLK), jnp.bfloat16),
            pltpu.VMEM((2, 256, PIV), jnp.bfloat16),
            pltpu.VMEM((256, NBL * BLK), jnp.float32),
            pltpu.VMEM((2, 256 * NBL, BLK), jnp.bfloat16),
            pltpu.VMEM((BLK * NBL, BLK), jnp.float32),
            small, small, small,
            pltpu.VMEM((128 * CAP, BLK), jnp.int32),
            pltpu.VMEM((8, BLK), jnp.int32),
            pltpu.SMEM((8, BLK), jnp.int32),
            dma((4, 3)), dma((4, 3)), dma((4, 3)),
            dma((40,)), dma((40,)), dma,
            dma((4,)), dma, dma, dma((2,)), dma((2,)),
        ],
        compiler_params=pltpu.CompilerParams(
            collective_id=0, has_side_effects=True, vmem_limit_bytes=58 * 2**20
        ),
        name="front",
    )(table, size, pattern, blocks, meta, front, pivot, panel)[0]


def per_device(
    front_entries,
    contributions,
    dest_owner,
    dest_row,
    dest_col,
    pivot_inverse,
    panel,
    pattern,
    front_size,
):
    devices = lax.axis_size("front") * lax.axis_size("grid")
    count = contributions.shape[0]
    total_rows = front_entries.shape[1]
    sentinel = total_rows // BLK * NBL
    owner = dest_owner[:, 0]
    position = jnp.arange(count, dtype=jnp.int32)
    same_owner = owner[:, None] == owner[None, :]
    before = position[None, :] < position[:, None]
    ranking = jnp.sum((same_owner & before).astype(jnp.int32), axis=1)
    slots = owner * CAP + ranking
    table = jnp.zeros((devices * CAP,), jnp.int32).at[slots].set(position)
    targets = (
        jnp.full((devices * CAP,), sentinel, jnp.int32).at[slots].set(dest_row * NBL + dest_col)
    )
    meta = jnp.broadcast_to(targets.reshape(8, 4, 4, CAP, 1), (8, 4, 4, CAP, BLK))
    out = schur_of_front(
        table,
        front_size,
        pattern[0, :, :, 0],
        contributions,
        meta,
        front_entries.reshape(total_rows * NBL, BLK),
        pivot_inverse[0],
        panel[0],
    )
    return out.reshape(1, -1, NBL, BLK)


def solution(mesh):
    placed = (
        P("front", None, None, "grid"),
        P(("front", "grid"), None, None),
        P(("front", "grid"), None),
        P(("front", "grid")),
        P(("front", "grid")),
        P("front", None, None),
        P("front", "grid", None),
        P("front", None, None, "grid"),
        P("front"),
    )
    return jax.shard_map(
        per_device,
        mesh=mesh,
        in_specs=placed,
        out_specs=P("front", None, None, "grid"),
        check_vma=False,
    )
```

```python
import functools

import jax
import jax.numpy as jnp
from jax import lax
from jax.experimental import pallas as pl
from jax.experimental.pallas import tpu as pltpu
from jax.sharding import PartitionSpec as P

BLK = 128
PIV = 1024
NBL = 4
CAP = 2
MESH = pl.DeviceIdType.MESH
PARTS = ((0, 96), (96, 80), (176, 80))
DEPTH = 4
ORDERS = ((0, 1, 2), (1, 2, 0), (2, 0, 1))


def at_axis(axis, where, rows=None):
    index = [slice(None)] * 5
    index[axis] = where
    if rows is not None:
        index[3] = pl.ds(rows[0], rows[1])
    return tuple(index)


def front_kernel(
    size, pattern, owner, spots, blocks, front, pivot, panel,
    out, arrived, panel_full,
    slots, stage1, stage2, blocks_v, sums, pivot_v, top, factor, panel_v,
    update0, update1, wide0, wide1,
    m0, m1, m2, m3, places, chain_v, chain,
    send_sem, recv_sem, own_sem, gsend_sem, grecv_sem,
    load_sem, lower_sem, arrived_sem, chain_sem, panel_sem, out_sem,
):
    f = lax.axis_index("front")
    g = lax.axis_index("grid")
    y, z = g // 4, g % 4
    me = (f, y, z)

    def device(axis, coordinate):
        if axis == 0:
            return (coordinate, g)
        if axis == 1:
            return (f, coordinate * 4 + z)
        return (f, y * 4 + coordinate)

    def peer(axis, d):
        if axis == 0:
            return ((f // 2 + d // 2) % 4) * 2 + (f + d) % 2
        return (me[axis] + d) % 4

    offsets = ((2, 6, 4, 3, 7, 5, 1), (1, 3, 2), (1, 3, 2))

    barrier = pltpu.get_barrier_semaphore()
    for axis in range(3):
        for d in offsets[axis]:
            pl.semaphore_signal(
                barrier, inc=1, device_id=device(axis, peer(axis, d)), device_id_type=MESH
            )

    load_blocks = pltpu.make_async_copy(blocks, blocks_v, load_sem.at[0])
    load_top = pltpu.make_async_copy(front.at[0], stage1.at[0], load_sem.at[1])
    load_pivot = pltpu.make_async_copy(pivot, pivot_v, load_sem.at[2])
    load_lower = [
        pltpu.make_async_copy(front.at[1 + i], slots.at[i], lower_sem.at[i]) for i in range(8)
    ]
    load_blocks.start()

    def make_slots():
        shape = (128, owner.shape[1])
        whose = lax.broadcasted_iota(jnp.int32, shape, 0)
        block = lax.broadcasted_iota(jnp.int32, shape, 1)
        spot = jnp.broadcast_to(spots[...], shape)
        match = jnp.broadcast_to(owner[...], shape) == whose
        first = jnp.min(jnp.where(match, block, shape[1]), axis=1, keepdims=True)
        second = jnp.max(jnp.where(match, block, -1), axis=1, keepdims=True)
        nowhere = front.shape[0] * 16 * CAP
        square = (128, BLK)
        for j, (chosen, there) in enumerate(
            ((first, second >= 0), (second, second > first))
        ):
            hit = jnp.max(jnp.where(block == chosen, spot, 0), axis=1, keepdims=True)
            hit = jnp.where(there, hit, nowhere)
            places[pl.ds(j, 128, stride=CAP), :] = jnp.broadcast_to(hit, square)
            index = jnp.broadcast_to(jnp.where(there, chosen, 0), square)
            diagonal = lax.broadcasted_iota(jnp.int32, square, 0) == lax.broadcasted_iota(
                jnp.int32, square, 1
            )
            chain_v[j : j + 1, :] = jnp.sum(
                jnp.where(diagonal, index, 0), axis=0, keepdims=True
            )
        copy = pltpu.make_async_copy(chain_v, chain, chain_sem)
        copy.start()

        def spread(d, carry):
            m0[d // 16, (d // 4) % 4, d % 4] = places[pl.ds(d * CAP, CAP), :]
            return carry

        lax.fori_loop(0, 128, spread, 0)
        copy.wait()

    def fill(d, carry):
        for j in range(CAP):
            slots[d // 16, (d // 4) % 4, d % 4, pl.ds(j * BLK, BLK), :] = blocks_v[chain[j, d]]
        return carry

    chains = []
    for part, (rows, order) in enumerate(zip(PARTS, ORDERS)):
        chains.append(((slots, rows), (stage1, rows), (stage2, rows), (arrived, rows), order))
    chains.append(((m0, None), (m1, None), (m2, None), (m3, None), (0, 1, 2)))

    def view(buffer, axis, where):
        ref, rows = buffer
        return ref.at[at_axis(axis, where, rows)]

    pending = {}

    def start(part, stage):
        steps = chains[part]
        source, target, axis = steps[stage], steps[stage + 1], steps[4][stage]
        own = pltpu.make_async_copy(
            view(source, axis, me[axis]), view(target, axis, me[axis]), own_sem.at[part, stage]
        )
        own.start()
        for d in offsets[axis]:
            there = peer(axis, d)
            pltpu.make_async_remote_copy(
                src_ref=view(source, axis, there),
                dst_ref=view(target, axis, me[axis]),
                send_sem=send_sem.at[part, stage],
                recv_sem=recv_sem.at[part, stage],
                device_id=device(axis, there),
                device_id_type=MESH,
            ).start()
        count = len(offsets[axis])
        whole = pltpu.make_async_remote_copy(
            src_ref=view(source, axis, pl.ds(0, count)),
            dst_ref=view(target, axis, pl.ds(0, count)),
            send_sem=send_sem.at[part, stage],
            recv_sem=recv_sem.at[part, stage],
            device_id=device(axis, peer(axis, 1)),
            device_id_type=MESH,
        )
        pending[part, stage] = (own, whole)

    def finish(part, stage):
        own, whole = pending[part, stage]
        own.wait()
        whole.wait_recv()

    gathers = []
    got = {}

    def place(half, dp, ds):
        if half == 0:
            return (y + dp + 4) % 4, (z + ds + 4) % 4
        return (y + ds + 4) % 4, (z + dp + 4) % 4

    def give(key, half, dp, ds, piece, along, step):
        py, pz = place(half, dp, ds)
        first, count = half * 256, 256
        if piece is not None:
            first, count = first + 128 * piece, 128
        rows = pl.ds(first, count)
        axis = (1, 2)[half] if along == 0 else (2, 1)[half]
        source = panel.at[rows] if (dp, ds) == (0, 0) else panel_full.at[py, pz, rows]
        index = len(gathers)
        copy = pltpu.make_async_remote_copy(
            src_ref=source,
            dst_ref=panel_full.at[py, pz, rows],
            send_sem=gsend_sem.at[index],
            recv_sem=grecv_sem.at[index],
            device_id=device(axis, peer(axis, step % 4)),
            device_id_type=MESH,
        )
        copy.start()
        gathers.append(copy)
        got[key] = copy

    def each(act):
        for half in (0, 1):
            for step, piece in ((1, 0), (-1, 1)):
                act(half, step, piece)

    def first_line():
        each(lambda h, s, p: give((h, "p", s), h, 0, 0, None, 0, s))

    def second_line(dp):
        each(lambda h, s, p: give((h, "s", dp, s), h, dp, 0, None, 1, s))

    def first_forward():
        each(lambda h, s, p: got[h, "p", s].wait_recv())
        each(lambda h, s, p: give((h, "pf", s), h, -s, 0, p, 0, s))

    def second_forward(dp):
        each(lambda h, s, p: got[h, "s", dp, s].wait_recv())
        each(lambda h, s, p: give((h, "sf", dp, s), h, dp, -s, p, 1, s))

    def landed(kind, *rest):
        each(lambda h, s, p: got[(h, kind) + rest + (s,)].wait_recv())

    def make_tables():
        def spread(d, carry):
            places[pl.ds(d * CAP, CAP), :] = m3[d // 16, (d // 4) % 4, d % 4]
            return carry

        lax.fori_loop(0, 128, spread, 0)
        where = places[...]
        slot = lax.broadcasted_iota(jnp.int32, where.shape, 0)
        lane = lax.broadcasted_iota(jnp.int32, where.shape, 1)

        def latest(same):
            found = jnp.max(jnp.where(same, slot, -1), axis=0, keepdims=True)
            return jnp.where(found < 0, CAP * 128, found)

        for half in range(2):
            mine = lane + half * BLK
            along = jnp.sum(jnp.where(slot == mine, where, 0), axis=0, keepdims=True)
            same = jnp.logical_and(where == along, slot < mine)
            chain_v[half : half + 1, :] = latest(same)
        for third in range(3):
            same = where == lane + third * BLK
            chain_v[2 + third : 3 + third, :] = latest(same)
        copy = pltpu.make_async_copy(chain_v, chain, chain_sem)
        copy.start()
        copy.wait()

    def block_of(t):
        d = t // CAP
        return slots[d // 16, (d // 4) % 4, d % 4, pl.ds((t % CAP) * BLK, BLK), :].astype(
            jnp.float32
        )

    count = sums.shape[0] - 1

    def add_up(arrivals):
        sums[count] = jnp.zeros((BLK, BLK), jnp.float32)

        def one(t, carry):
            sums[t] = block_of(t) + sums[chain[t // BLK, t % BLK]]
            return carry

        each_time = count // len(arrivals)
        for i, copy in enumerate(arrivals):
            copy.wait()
            lax.fori_loop(i * each_time, (i + 1) * each_time, one, 0)

    def assembled(source, row):
        d = 2 * row % 16
        for i, wide in enumerate((wide0, wide1)):
            wide[pl.ds(0, 256), :] = source[d // 4, d % 4 + i].astype(jnp.float32)
        values = []
        for k in range(NBL):
            p = row * NBL + k
            total = sums[chain[2 + p // BLK, p % BLK]]
            part = pl.ds(k, BLK // 2, stride=NBL)
            value = jnp.concatenate([wide0[part, :], wide1[part, :]], axis=0)
            values.append((value + total).astype(jnp.bfloat16))
        return d, values

    def make_factor():
        def one(row, carry):
            _, values = assembled(stage1.at[0], row)
            for k in range(NBL):
                top[pl.ds(row * BLK, BLK), pl.ds(k * BLK, BLK)] = values[k]
            return carry

        lax.fori_loop(0, PIV // BLK, one, 0)
        load_pivot.wait()
        factor[...] = jnp.dot(
            pivot_v[...], top[...], preferred_element_type=jnp.float32
        ).astype(jnp.bfloat16)

    def make_lower():
        for i in range(8):
            load_lower[i].wait()

            def one(j, carry):
                d, values = assembled(slots.at[i], PIV // BLK + i * 8 + j)
                for k in range(NBL):
                    slots[i, d // 4, d % 4 + k // 2, pl.ds(k % 2 * BLK, BLK), :] = values[k]
                return carry

            lax.fori_loop(0, 8, one, 0)

    limit = size[0]

    def load(i, half, decode):
        rows = pl.ds(half * 256, 256)
        if decode is None:
            source = panel.at[rows]
        else:
            py, pz = decode(i, half)
            source = panel_full.at[py, pz, rows]
        return pltpu.make_async_copy(
            source, panel_v.at[i % DEPTH, half], panel_sem.at[i % DEPTH, half]
        )

    def prefetch(first, count, decode):
        for i in range(min(DEPTH, count)):
            for half in (0, 1):
                load(first + i, half, None if first + i == 0 else decode).start()

    def updates(first, count, decode):
        def one(i, carry):
            for half, update in ((0, update0), (1, update1)):
                load(i, half, decode).wait()
                update[...] = jnp.dot(
                    panel_v[i % DEPTH, half], factor[...], preferred_element_type=jnp.float32
                )
            for half, update in ((0, update0), (1, update1)):
                py, pz = decode(i, half)
                for j, wide in ((0, wide0), (1, wide1)):
                    row = (py * 4 + pz) * 4 + half * 2 + j
                    d = 2 * row
                    for k in range(NBL):
                        keep = jnp.logical_and(row < limit, k * 16 + g < limit)
                        chosen = pattern[k, 0, row].astype(jnp.float32)
                        lower = slots[
                            d // 16, (d // 4) % 4, d % 4 + k // 2, pl.ds(k % 2 * BLK, BLK), :
                        ].astype(jnp.float32)
                        taken = update[pl.ds(j * BLK, BLK), pl.ds(k * BLK, BLK)]
                        wide[pl.ds(k, BLK, stride=NBL), :] = jnp.where(
                            keep, lower - chosen * taken, 0.0
                        )
                    for part in range(2):
                        stage2[i // 2, i % 2 * 2 + half, 2 * j + part] = wide[
                            pl.ds(part * 256, 256), :
                        ].astype(jnp.bfloat16)
                pltpu.make_async_copy(
                    stage2.at[i // 2, i % 2 * 2 + half],
                    out.at[pl.ds((py * 4 + pz) * 8 + half * 4, 4)],
                    out_sem,
                ).start()

            if count > DEPTH:

                @pl.when(i + DEPTH < first + count)
                def _():
                    for half in (0, 1):
                        load(i + DEPTH, half, decode).start()

            return carry

        lax.fori_loop(first, first + count, one, 0)

    def spot(half, dp, ds):
        return (y + dp * (1 - half) + ds * half) % 4, (z + dp * half + ds * (1 - half)) % 4

    def near(i, half):
        a, b = i % 3, i // 3
        return spot(half, a + a // 2, b + b // 2)

    def far(i, half):
        a, b = (i - 9) % 3, (i - 9) // 3
        d = a + a // 2
        return spot(half, d * (1 - b) + 2 * b, d * b + 2 * (1 - b))

    def last(i, half):
        return spot(half, 2, 2)

    pl.semaphore_wait(barrier, 13)
    first_line()
    second_line(0)
    load_pivot.start()
    make_slots()
    start(3, 0)
    load_blocks.wait()
    lax.fori_loop(0, 128, fill, 0)
    for part in range(3):
        start(part, 0)
    finish(3, 0)
    start(3, 1)
    for part in range(3):
        finish(part, 0)
        start(part, 1)
    finish(3, 1)
    start(3, 2)
    first_forward()
    second_forward(0)
    for part in range(3):
        finish(part, 1)
        start(part, 2)
    second_line(-1)
    finish(3, 2)
    make_tables()
    for part in range(3):
        pending[part, 0][1].wait_send()
        pending[part, 1][1].wait_send()
    load_top.start()
    for part in range(3):
        finish(part, 2)
    back = [
        pltpu.make_async_copy(arrived.at[i], slots.at[i], arrived_sem.at[i]) for i in range(8)
    ]
    for copy in back:
        copy.start()
    second_line(1)
    landed("pf")
    second_line(2)
    second_forward(-1)
    add_up(back)
    for copy in load_lower:
        copy.start()
    second_forward(1)
    prefetch(0, 9, near)
    load_top.wait()
    make_factor()
    make_lower()
    second_forward(2)
    for part in range(3):
        pending[part, 2][1].wait_send()
    updates(0, 9, near)
    for dp in (0, -1, 1):
        landed("sf", dp)
    prefetch(9, 6, far)
    updates(9, 6, far)
    landed("sf", 2)
    prefetch(15, 1, last)
    updates(15, 1, last)
    pltpu.make_async_copy(stage2, arrived, out_sem).wait()
    for (part, stage), (_, whole) in pending.items():
        if part == 3:
            whole.wait_send()
    for copy in gathers:
        copy.wait_send()


def schur_of_front(size, pattern, owner, spots, blocks, front, pivot, panel):
    grid_of = (8, 4, 4)
    any_space = pl.BlockSpec(memory_space=pl.ANY)
    smem = pl.BlockSpec(memory_space=pltpu.SMEM)
    vmem = pl.BlockSpec(memory_space=pltpu.VMEM)
    dma = pltpu.SemaphoreType.DMA
    outs = [
        (128, CAP * BLK, BLK),
        grid_of + (CAP * BLK, BLK),
        (4, 4) + panel.shape,
    ]
    small = pltpu.VMEM(grid_of + (CAP, BLK), jnp.int32)
    large = pltpu.VMEM(grid_of + (CAP * BLK, BLK), jnp.bfloat16)
    return pl.pallas_call(
        front_kernel,
        out_shape=[jax.ShapeDtypeStruct(shape, jnp.bfloat16) for shape in outs],
        in_specs=[smem, smem, vmem, vmem, any_space, any_space, any_space, any_space],
        out_specs=[any_space] * len(outs),
        scratch_shapes=[
            large, large, large,
            pltpu.VMEM(blocks.shape, jnp.bfloat16),
            pltpu.VMEM((128 * CAP + 1, BLK, BLK), jnp.float32),
            pltpu.VMEM(pivot.shape, jnp.bfloat16),
            pltpu.VMEM((PIV, NBL * BLK), jnp.bfloat16),
            pltpu.VMEM((PIV, NBL * BLK), jnp.bfloat16),
            pltpu.VMEM((DEPTH, 2, 256, PIV), jnp.bfloat16),
            pltpu.VMEM((256, NBL * BLK), jnp.float32),
            pltpu.VMEM((256, NBL * BLK), jnp.float32),
            pltpu.VMEM((BLK * NBL, BLK), jnp.float32),
            pltpu.VMEM((BLK * NBL, BLK), jnp.float32),
            small, small, small, small,
            pltpu.VMEM((128 * CAP, BLK), jnp.int32),
            pltpu.VMEM((8, BLK), jnp.int32),
            pltpu.SMEM((8, BLK), jnp.int32),
            dma((4, 3)), dma((4, 3)), dma((4, 3)),
            dma((40,)), dma((40,)),
            dma((3,)), dma((8,)), dma((8,)), dma, dma((DEPTH, 2)), dma,
        ],
        compiler_params=pltpu.CompilerParams(
            collective_id=0, has_side_effects=True, vmem_limit_bytes=62 * 2**20
        ),
        name="front",
    )(size, pattern, owner, spots, blocks, front, pivot, panel)[0]


PIECES = 8


def pass_kernel(source, target, held, in_sem, out_sem):
    rows = source.shape[0] // PIECES
    steps = []
    for i in range(PIECES):
        part = pl.ds(i * rows, rows)
        steps.append(
            (
                pltpu.make_async_copy(source.at[part], held.at[part], in_sem.at[i]),
                pltpu.make_async_copy(held.at[part], target.at[part], out_sem.at[i]),
            )
        )
    for take, _ in steps:
        take.start()
    for take, give in steps:
        take.wait()
        give.start()
    for _, give in steps:
        give.wait()


def pass_on(array):
    any_space = pl.BlockSpec(memory_space=pl.ANY)
    return pl.pallas_call(
        pass_kernel,
        out_shape=jax.ShapeDtypeStruct(array.shape, array.dtype),
        in_specs=[any_space],
        out_specs=any_space,
        scratch_shapes=[
            pltpu.VMEM(array.shape, array.dtype),
            pltpu.SemaphoreType.DMA((PIECES,)),
            pltpu.SemaphoreType.DMA((PIECES,)),
        ],
        compiler_params=pltpu.CompilerParams(vmem_limit_bytes=60 * 2**20),
        name="pass_on",
    )(array)


def per_device(
    front_entries,
    contributions,
    dest_owner,
    dest_row,
    dest_col,
    pivot_inverse,
    panel,
    pattern,
    front_size,
):
    out = schur_of_front(
        front_size,
        pattern[0, :, :, 0].T.reshape(NBL, 1, -1),
        dest_owner.reshape(1, -1),
        (dest_row * NBL + dest_col).reshape(1, -1),
        contributions,
        front_entries.reshape(-1, 4, 4, CAP * BLK, BLK),
        pivot_inverse[0],
        panel[0],
    )
    out = pass_on(out)
    return out.reshape(1, -1, NBL, BLK)


def solution(mesh):
    placed = (
        P("front", None, None, "grid"),
        P(("front", "grid"), None, None),
        P(("front", "grid"), None),
        P(("front", "grid")),
        P(("front", "grid")),
        P("front", None, None),
        P("front", "grid", None),
        P("front", None, None, "grid"),
        P("front"),
    )
    return jax.shard_map(
        per_device,
        mesh=mesh,
        in_specs=placed,
        out_specs=P("front", None, None, "grid"),
        check_vma=False,
    )
```

```python
import functools

import jax
import jax.numpy as jnp
from jax import lax
from jax.experimental import pallas as pl
from jax.experimental.pallas import tpu as pltpu
from jax.sharding import PartitionSpec as P

BLK = 128
PIV = 1024
NBL = 4
CAP = 2
MESH = pl.DeviceIdType.MESH
PARTS = ((0, 96), (96, 80), (176, 80))
DEPTH = 4
ORDERS = ((0, 1, 2), (1, 2, 0), (2, 0, 1))


def at_axis(axis, where, rows=None):
    index = [slice(None)] * 5
    index[axis] = where
    if rows is not None:
        index[3] = pl.ds(rows[0], rows[1])
    return tuple(index)


def schur_rows(update, wides, lower, write, pattern, limit, column, first):
    for j, wide in enumerate(wides):
        row = first + j
        for k in range(NBL):
            keep = jnp.logical_and(row < limit, k * 16 + column < limit)
            chosen = pattern[k, 0, row].astype(jnp.float32)
            taken = update[pl.ds(j * BLK, BLK), pl.ds(k * BLK, BLK)]
            here = lower(row, k).astype(jnp.float32)
            wide[pl.ds(k, BLK, stride=NBL), :] = jnp.where(keep, here - chosen * taken, 0.0)
        for part in range(2):
            write(row * 2 + part, wide[pl.ds(part * 256, 256), :].astype(jnp.bfloat16))


def front_kernel(
    size, pattern, owner, rows_to, cols_to, blocks, front, pivot, panel,
    out, arrived, panel_full, factor,
    slots, stage1, blocks_v, sums, pivot_v, top, panel_v,
    update0, update1, wide0, wide1,
    m0, m1, m2, m3, places, chain_v, chain,
    send_sem, recv_sem, own_sem, gsend_sem, grecv_sem,
    load_sem, lower_sem, arrived_sem, chain_sem, panel_sem, leave_sem,
):
    f = lax.axis_index("front")
    g = lax.axis_index("grid")
    y, z = g // 4, g % 4
    me = (f, y, z)

    def device(axis, coordinate):
        if axis == 0:
            return (coordinate, g)
        if axis == 1:
            return (f, coordinate * 4 + z)
        return (f, y * 4 + coordinate)

    def peer(axis, d):
        if axis == 0:
            return ((f // 2 + d // 2) % 4) * 2 + (f + d) % 2
        return (me[axis] + d) % 4

    offsets = ((2, 6, 4, 3, 7, 5, 1), (1, 3, 2), (1, 3, 2))

    barrier = pltpu.get_barrier_semaphore()
    for axis in range(3):
        for d in offsets[axis]:
            pl.semaphore_signal(
                barrier, inc=1, device_id=device(axis, peer(axis, d)), device_id_type=MESH
            )

    load_blocks = pltpu.make_async_copy(blocks, blocks_v, load_sem.at[0])
    load_top = pltpu.make_async_copy(front.at[0], stage1.at[0], load_sem.at[1])
    load_pivot = pltpu.make_async_copy(pivot, pivot_v, load_sem.at[2])
    load_lower = [
        pltpu.make_async_copy(front.at[1 + i], slots.at[i], lower_sem.at[i]) for i in range(8)
    ]
    load_blocks.start()

    def make_slots():
        shape = (128, owner.shape[1])
        whose = lax.broadcasted_iota(jnp.int32, shape, 0)
        block = lax.broadcasted_iota(jnp.int32, shape, 1)
        spot = jnp.broadcast_to(rows_to[...] * NBL + cols_to[...], shape)
        match = jnp.broadcast_to(owner[...], shape) == whose
        first = jnp.min(jnp.where(match, block, shape[1]), axis=1, keepdims=True)
        second = jnp.max(jnp.where(match, block, -1), axis=1, keepdims=True)
        nowhere = front.shape[0] * 16 * CAP
        square = (128, BLK)
        for j, (chosen, there) in enumerate(
            ((first, second >= 0), (second, second > first))
        ):
            hit = jnp.max(jnp.where(block == chosen, spot, 0), axis=1, keepdims=True)
            hit = jnp.where(there, hit, nowhere)
            places[pl.ds(j, 128, stride=CAP), :] = jnp.broadcast_to(hit, square)
            index = jnp.broadcast_to(jnp.where(there, chosen, 0), square)
            diagonal = lax.broadcasted_iota(jnp.int32, square, 0) == lax.broadcasted_iota(
                jnp.int32, square, 1
            )
            chain_v[j : j + 1, :] = jnp.sum(
                jnp.where(diagonal, index, 0), axis=0, keepdims=True
            )
        copy = pltpu.make_async_copy(chain_v, chain, chain_sem)
        copy.start()

        def spread(d, carry):
            m0[d // 16, (d // 4) % 4, d % 4] = places[pl.ds(d * CAP, CAP), :]
            return carry

        lax.fori_loop(0, 128, spread, 0)
        copy.wait()

    def fill(d, carry):
        for j in range(CAP):
            slots[d // 16, (d // 4) % 4, d % 4, pl.ds(j * BLK, BLK), :] = blocks_v[chain[j, d]]
        return carry

    chains = []
    for part, (rows, order) in enumerate(zip(PARTS, ORDERS)):
        chains.append(((slots, rows), (stage1, rows), (out, rows), (arrived, rows), order))
    chains.append(((m0, None), (m1, None), (m2, None), (m3, None), (0, 1, 2)))

    def view(buffer, axis, where):
        ref, rows = buffer
        return ref.at[at_axis(axis, where, rows)]

    pending = {}

    def start(part, stage):
        steps = chains[part]
        source, target, axis = steps[stage], steps[stage + 1], steps[4][stage]
        own = pltpu.make_async_copy(
            view(source, axis, me[axis]), view(target, axis, me[axis]), own_sem.at[part, stage]
        )
        own.start()
        for d in offsets[axis]:
            there = peer(axis, d)
            pltpu.make_async_remote_copy(
                src_ref=view(source, axis, there),
                dst_ref=view(target, axis, me[axis]),
                send_sem=send_sem.at[part, stage],
                recv_sem=recv_sem.at[part, stage],
                device_id=device(axis, there),
                device_id_type=MESH,
            ).start()
        count = len(offsets[axis])
        whole = pltpu.make_async_remote_copy(
            src_ref=view(source, axis, pl.ds(0, count)),
            dst_ref=view(target, axis, pl.ds(0, count)),
            send_sem=send_sem.at[part, stage],
            recv_sem=recv_sem.at[part, stage],
            device_id=device(axis, peer(axis, 1)),
            device_id_type=MESH,
        )
        pending[part, stage] = (own, whole)

    def finish(part, stage):
        own, whole = pending[part, stage]
        own.wait()
        whole.wait_recv()

    gathers = []
    got = {}

    def place(half, dp, ds):
        if half == 0:
            return (y + dp + 4) % 4, (z + ds + 4) % 4
        return (y + ds + 4) % 4, (z + dp + 4) % 4

    def give(key, half, dp, ds, piece, along, step):
        py, pz = place(half, dp, ds)
        first, count = half * 256, 256
        if piece is not None:
            first, count = first + 128 * piece, 128
        rows = pl.ds(first, count)
        axis = (1, 2)[half] if along == 0 else (2, 1)[half]
        source = panel.at[rows] if (dp, ds) == (0, 0) else panel_full.at[py, pz, rows]
        index = len(gathers)
        copy = pltpu.make_async_remote_copy(
            src_ref=source,
            dst_ref=panel_full.at[py, pz, rows],
            send_sem=gsend_sem.at[index],
            recv_sem=grecv_sem.at[index],
            device_id=device(axis, peer(axis, step % 4)),
            device_id_type=MESH,
        )
        copy.start()
        gathers.append(copy)
        got[key] = copy

    def each(act):
        for half in (0, 1):
            for step, piece in ((1, 0), (-1, 1)):
                act(half, step, piece)

    def first_line():
        each(lambda h, s, p: give((h, "p", s), h, 0, 0, None, 0, s))

    def second_line(dp):
        each(lambda h, s, p: give((h, "s", dp, s), h, dp, 0, None, 1, s))

    def first_forward():
        each(lambda h, s, p: got[h, "p", s].wait_recv())
        each(lambda h, s, p: give((h, "pf", s), h, -s, 0, p, 0, s))

    def second_forward(dp):
        each(lambda h, s, p: got[h, "s", dp, s].wait_recv())
        each(lambda h, s, p: give((h, "sf", dp, s), h, dp, -s, p, 1, s))

    def landed(kind, *rest):
        each(lambda h, s, p: got[(h, kind) + rest + (s,)].wait_recv())

    def make_tables():
        def spread(d, carry):
            places[pl.ds(d * CAP, CAP), :] = m3[d // 16, (d // 4) % 4, d % 4]
            return carry

        lax.fori_loop(0, 128, spread, 0)
        where = places[...]
        slot = lax.broadcasted_iota(jnp.int32, where.shape, 0)
        lane = lax.broadcasted_iota(jnp.int32, where.shape, 1)

        def latest(same):
            found = jnp.max(jnp.where(same, slot, -1), axis=0, keepdims=True)
            return jnp.where(found < 0, CAP * 128, found)

        for half in range(2):
            mine = lane + half * BLK
            along = jnp.sum(jnp.where(slot == mine, where, 0), axis=0, keepdims=True)
            same = jnp.logical_and(where == along, slot < mine)
            chain_v[half : half + 1, :] = latest(same)
        for third in range(3):
            same = where == lane + third * BLK
            chain_v[2 + third : 3 + third, :] = latest(same)
        copy = pltpu.make_async_copy(chain_v, chain, chain_sem)
        copy.start()
        copy.wait()

    def block_of(t):
        d = t // CAP
        return slots[d // 16, (d // 4) % 4, d % 4, pl.ds((t % CAP) * BLK, BLK), :].astype(
            jnp.float32
        )

    count = sums.shape[0] - 1

    def add_up(arrivals):
        sums[count] = jnp.zeros((BLK, BLK), jnp.float32)

        def one(t, carry):
            sums[t] = block_of(t) + sums[chain[t // BLK, t % BLK]]
            return carry

        each_time = count // len(arrivals)
        for i, copy in enumerate(arrivals):
            copy.wait()
            lax.fori_loop(i * each_time, (i + 1) * each_time, one, 0)

    def assembled(source, row):
        d = 2 * row % 16
        for i, wide in enumerate((wide0, wide1)):
            wide[pl.ds(0, 256), :] = source[d // 4, d % 4 + i].astype(jnp.float32)
        values = []
        for k in range(NBL):
            p = row * NBL + k
            total = sums[chain[2 + p // BLK, p % BLK]]
            part = pl.ds(k, BLK // 2, stride=NBL)
            value = jnp.concatenate([wide0[part, :], wide1[part, :]], axis=0)
            values.append((value + total).astype(jnp.bfloat16))
        return d, values

    def make_factor():
        def one(row, carry):
            _, values = assembled(stage1.at[0], row)
            for k in range(NBL):
                top[pl.ds(row * BLK, BLK), pl.ds(k * BLK, BLK)] = values[k]
            return carry

        lax.fori_loop(0, PIV // BLK, one, 0)
        load_pivot.wait()
        factor[...] = jnp.dot(
            pivot_v[...], top[...], preferred_element_type=jnp.float32
        ).astype(jnp.bfloat16)

    def make_lower():
        for i in range(8):
            load_lower[i].wait()

            def one(j, carry):
                d, values = assembled(slots.at[i], PIV // BLK + i * 8 + j)
                for k in range(NBL):
                    slots[i, d // 4, d % 4 + k // 2, pl.ds(k % 2 * BLK, BLK), :] = values[k]
                return carry

            lax.fori_loop(0, 8, one, 0)

    limit = size[0]

    def load(i, half, decode):
        rows = pl.ds(half * 256, 256)
        if decode is None:
            source = panel.at[rows]
        else:
            py, pz = decode(i, half)
            source = panel_full.at[py, pz, rows]
        return pltpu.make_async_copy(
            source, panel_v.at[i % DEPTH, half], panel_sem.at[i % DEPTH, half]
        )

    def prefetch(first, count, decode):
        for i in range(min(DEPTH, count)):
            for half in (0, 1):
                load(first + i, half, None if first + i == 0 else decode).start()

    def updates(first, count, decode):
        def lower(row, k):
            d = 2 * row
            return slots[d // 16, (d // 4) % 4, d % 4 + k // 2, pl.ds(k % 2 * BLK, BLK), :]

        def write(d, value):
            out[d // 16, (d // 4) % 4, d % 4] = value

        def one(i, carry):
            for half, update in ((0, update0), (1, update1)):
                load(i, half, decode).wait()
                update[...] = jnp.dot(
                    panel_v[i % DEPTH, half], factor[...], preferred_element_type=jnp.float32
                )
            for half, update in ((0, update0), (1, update1)):
                py, pz = decode(i, half)
                first_row = (py * 4 + pz) * 4 + half * 2
                schur_rows(update, (wide0, wide1), lower, write, pattern, limit, g, first_row)

            if count > DEPTH:

                @pl.when(i + DEPTH < first + count)
                def _():
                    for half in (0, 1):
                        load(i + DEPTH, half, decode).start()

            return carry

        lax.fori_loop(first, first + count, one, 0)

    def spot(half, dp, ds):
        return (y + dp * (1 - half) + ds * half) % 4, (z + dp * half + ds * (1 - half)) % 4

    def near(i, half):
        a, b = i % 3, i // 3
        return spot(half, a + a // 2, b + b // 2)

    def middle(i, half):
        return spot(half, 2 * (1 - (i - 9) // 3), (i - 6) % 4)

    def late(i, half):
        return spot(half, 3 - 2 * (i - 13), 2)

    pl.semaphore_wait(barrier, 13)
    first_line()
    second_line(0)
    load_pivot.start()
    make_slots()
    start(3, 0)
    load_blocks.wait()
    lax.fori_loop(0, 128, fill, 0)
    for part in range(3):
        start(part, 0)
    finish(3, 0)
    start(3, 1)
    for part in range(3):
        finish(part, 0)
        start(part, 1)
    finish(3, 1)
    start(3, 2)
    first_forward()
    second_forward(0)
    for part in range(3):
        finish(part, 1)
        start(part, 2)
    second_line(-1)
    finish(3, 2)
    make_tables()
    for part in range(3):
        pending[part, 0][1].wait_send()
        pending[part, 1][1].wait_send()
    load_top.start()
    for part in range(3):
        finish(part, 2)
    back = [
        pltpu.make_async_copy(arrived.at[i], slots.at[i], arrived_sem.at[i]) for i in range(8)
    ]
    for copy in back:
        copy.start()
    second_line(1)
    landed("pf")
    second_line(2)
    second_forward(-1)
    add_up(back)
    for copy in load_lower:
        copy.start()
    second_forward(1)
    prefetch(0, 9, near)
    load_top.wait()
    make_factor()
    make_lower()
    for part in range(3):
        pending[part, 2][1].wait_send()
    final = (y + 2) % 4 * 4 + (z + 2) % 4
    leave_rows = pltpu.make_async_copy(
        slots.at[final // 2, pl.ds(final % 2 * 2, 2)],
        out.at[final // 2, pl.ds(final % 2 * 2, 2)],
        leave_sem,
    )
    leave_rows.start()
    updates(0, 9, near)
    second_forward(2)
    landed("sf", 0)
    prefetch(9, 4, middle)
    updates(9, 4, middle)
    for i, dp in ((13, -1), (14, 1)):
        landed("sf", dp)
        prefetch(i, 1, late)
        updates(i, 1, late)
    leave_rows.wait()
    landed("sf", 2)
    for (part, stage), (_, whole) in pending.items():
        if part == 3:
            whole.wait_send()
    for copy in gathers:
        copy.wait_send()


def front_parts(size, pattern, owner, rows_to, cols_to, blocks, front, pivot, panel):
    grid_of = (8, 4, 4)
    any_space = pl.BlockSpec(memory_space=pl.ANY)
    smem = pl.BlockSpec(memory_space=pltpu.SMEM)
    vmem = pl.BlockSpec(memory_space=pltpu.VMEM)
    dma = pltpu.SemaphoreType.DMA
    outs = [
        pltpu.VMEM(grid_of + (CAP * BLK, BLK), jnp.bfloat16),
        jax.ShapeDtypeStruct(grid_of + (CAP * BLK, BLK), jnp.bfloat16),
        jax.ShapeDtypeStruct((4, 4) + panel.shape, jnp.bfloat16),
        pltpu.VMEM((PIV, NBL * BLK), jnp.bfloat16),
    ]
    small = pltpu.VMEM(grid_of + (CAP, BLK), jnp.int32)
    large = pltpu.VMEM(grid_of + (CAP * BLK, BLK), jnp.bfloat16)
    return pl.pallas_call(
        front_kernel,
        out_shape=outs,
        in_specs=[smem, smem, vmem, vmem, vmem] + [any_space] * 4,
        out_specs=[vmem, any_space, any_space, vmem],
        scratch_shapes=[
            large, large,
            pltpu.VMEM(blocks.shape, jnp.bfloat16),
            pltpu.VMEM((128 * CAP + 1, BLK, BLK), jnp.float32),
            pltpu.VMEM(pivot.shape, jnp.bfloat16),
            pltpu.VMEM((PIV, NBL * BLK), jnp.bfloat16),
            pltpu.VMEM((DEPTH, 2, 256, PIV), jnp.bfloat16),
            pltpu.VMEM((256, NBL * BLK), jnp.float32),
            pltpu.VMEM((256, NBL * BLK), jnp.float32),
            pltpu.VMEM((BLK * NBL, BLK), jnp.float32),
            pltpu.VMEM((BLK * NBL, BLK), jnp.float32),
            small, small, small, small,
            pltpu.VMEM((128 * CAP, BLK), jnp.int32),
            pltpu.VMEM((8, BLK), jnp.int32),
            pltpu.SMEM((8, BLK), jnp.int32),
            dma((4, 3)), dma((4, 3)), dma((4, 3)),
            dma((40,)), dma((40,)),
            dma((3,)), dma((8,)), dma((8,)), dma, dma((DEPTH, 2)), dma,
        ],
        compiler_params=pltpu.CompilerParams(
            collective_id=0, has_side_effects=True, vmem_limit_bytes=50 * 2**20
        ),
        name="front",
    )(size, pattern, owner, rows_to, cols_to, blocks, front, pivot, panel)


def last_kernel(
    size, pattern, parts, panel_full, factor, out,
    factor_v, panel_v, lower_v, update0, update1, result, wide0, wide1,
    load_sem, part_sem, out_sem,
):
    g = lax.axis_index("grid")
    final = (g // 4 + 2) % 4 * 4 + (g % 4 + 2) % 4
    loads = [
        pltpu.make_async_copy(factor, factor_v, load_sem.at[0]),
        pltpu.make_async_copy(panel_full.at[final // 4, final % 4], panel_v, load_sem.at[1]),
        pltpu.make_async_copy(parts.at[pl.ds(final * 8, 8)], lower_v, load_sem.at[2]),
    ]
    for copy in loads:
        copy.start()
    passed = []
    for i in range(1, 16):
        rows = pl.ds((final + i) % 16 * 8, 8)
        passed.append(pltpu.make_async_copy(parts.at[rows], out.at[rows], part_sem.at[i - 1]))
        passed[-1].start()
    for copy in loads:
        copy.wait()

    def lower(row, k):
        return lower_v[2 * (row - final * 4) + k // 2, pl.ds(k % 2 * BLK, BLK), :]

    def write(d, value):
        result[d - final * 8] = value

    for half, update in ((0, update0), (1, update1)):
        update[...] = jnp.dot(
            panel_v[pl.ds(half * 256, 256)], factor_v[...], preferred_element_type=jnp.float32
        )
    for half, update in ((0, update0), (1, update1)):
        first_row = final * 4 + half * 2
        schur_rows(update, (wide0, wide1), lower, write, pattern, size[0], g, first_row)
        done = pltpu.make_async_copy(
            result.at[pl.ds(half * 4, 4)],
            out.at[pl.ds(final * 8 + half * 4, 4)],
            out_sem.at[half],
        )
        done.start()
        passed.append(done)
    for copy in passed:
        copy.wait()


def last_part(size, pattern, parts, panel_full, factor):
    any_space = pl.BlockSpec(memory_space=pl.ANY)
    smem = pl.BlockSpec(memory_space=pltpu.SMEM)
    half = pltpu.VMEM((256, NBL * BLK), jnp.float32)
    wide = pltpu.VMEM((BLK * NBL, BLK), jnp.float32)
    rows = pltpu.VMEM((8, CAP * BLK, BLK), jnp.bfloat16)
    dma = pltpu.SemaphoreType.DMA
    return pl.pallas_call(
        last_kernel,
        out_shape=jax.ShapeDtypeStruct(parts.shape, parts.dtype),
        in_specs=[smem, smem] + [any_space] * 3,
        out_specs=any_space,
        scratch_shapes=[
            pltpu.VMEM(factor.shape, jnp.bfloat16),
            pltpu.VMEM(panel_full.shape[2:], jnp.bfloat16),
            rows, half, half, rows, wide, wide,
            dma((3,)), dma((15,)), dma((2,)),
        ],
        compiler_params=pltpu.CompilerParams(vmem_limit_bytes=36 * 2**20),
        name="last_part",
    )(size, pattern, parts, panel_full, factor)


def per_device(
    front_entries,
    contributions,
    dest_owner,
    dest_row,
    dest_col,
    pivot_inverse,
    panel,
    pattern,
    front_size,
):
    pattern = pattern[0, :, :, 0].T.reshape(NBL, 1, -1)
    parts, _, panel_full, factor = front_parts(
        front_size,
        pattern,
        dest_owner.reshape(1, -1),
        dest_row.reshape(1, -1),
        dest_col.reshape(1, -1),
        contributions,
        front_entries.reshape(-1, 4, 4, CAP * BLK, BLK),
        pivot_inverse[0],
        panel[0],
    )
    parts = parts.reshape(-1, CAP * BLK, BLK)
    out = last_part(front_size, pattern, parts, panel_full, factor)
    return out.reshape(1, -1, NBL, BLK)


def solution(mesh):
    placed = (
        P("front", None, None, "grid"),
        P(("front", "grid"), None, None),
        P(("front", "grid"), None),
        P(("front", "grid")),
        P(("front", "grid")),
        P("front", None, None),
        P("front", "grid", None),
        P("front", None, None, "grid"),
        P("front"),
    )
    return jax.shard_map(
        per_device,
        mesh=mesh,
        in_specs=placed,
        out_specs=P("front", None, None, "grid"),
        check_vma=False,
    )
```

```python
import functools

import jax
import jax.numpy as jnp
from jax import lax
from jax.experimental import pallas as pl
from jax.experimental.pallas import tpu as pltpu
from jax.sharding import PartitionSpec as P

BLK = 128
PIV = 1024
NBL = 4
CAP = 2
MESH = pl.DeviceIdType.MESH
PARTS = ((0, 96), (96, 80), (176, 80))
DEPTH = 4
ORDERS = ((0, 1, 2), (1, 2, 0), (2, 0, 1))


def at_axis(axis, where, rows=None):
    index = [slice(None)] * 5
    index[axis] = where
    if rows is not None:
        index[3] = pl.ds(rows[0], rows[1])
    return tuple(index)


def schur_rows(update, wides, lower, write, pattern, limit, column, first):
    for j, wide in enumerate(wides):
        row = first + j
        for k in range(NBL):
            keep = jnp.logical_and(row < limit, k * 16 + column < limit)
            chosen = pattern[k, 0, row].astype(jnp.float32)
            taken = update[pl.ds(j * BLK, BLK), pl.ds(k * BLK, BLK)]
            here = lower(row, k).astype(jnp.float32)
            wide[pl.ds(k, BLK, stride=NBL), :] = jnp.where(keep, here - chosen * taken, 0.0)
        for part in range(2):
            write(row * 2 + part, wide[pl.ds(part * 256, 256), :].astype(jnp.bfloat16))


def front_kernel(
    size, pattern, owner, rows_to, cols_to, blocks, front, pivot, panel,
    out, arrived, panel_full, factor,
    slots, stage1, blocks_v, sums, pivot_v, top, panel_v,
    update0, update1, wide0, wide1,
    m0, m1, m2, m3, places, chain_v, chain,
    send_sem, recv_sem, own_sem, gsend_sem, grecv_sem,
    load_sem, lower_sem, arrived_sem, chain_sem, panel_sem, leave_sem,
):
    f = lax.axis_index("front")
    g = lax.axis_index("grid")
    y, z = g // 4, g % 4
    me = (f, y, z)

    def device(axis, coordinate):
        if axis == 0:
            return (coordinate, g)
        if axis == 1:
            return (f, coordinate * 4 + z)
        return (f, y * 4 + coordinate)

    def peer(axis, d):
        if axis == 0:
            return ((f // 2 + d // 2) % 4) * 2 + (f + d) % 2
        return (me[axis] + d) % 4

    offsets = ((2, 6, 4, 3, 7, 5, 1), (1, 3, 2), (1, 3, 2))

    barrier = pltpu.get_barrier_semaphore()
    for axis in range(3):
        for d in offsets[axis]:
            pl.semaphore_signal(
                barrier, inc=1, device_id=device(axis, peer(axis, d)), device_id_type=MESH
            )

    load_blocks = pltpu.make_async_copy(blocks, blocks_v, load_sem.at[0])
    load_top = pltpu.make_async_copy(front.at[0], stage1.at[0], load_sem.at[1])
    load_pivot = pltpu.make_async_copy(pivot, pivot_v, load_sem.at[2])
    load_lower = [
        pltpu.make_async_copy(front.at[1 + i], slots.at[i], lower_sem.at[i]) for i in range(8)
    ]
    load_blocks.start()

    def make_slots():
        shape = (128, owner.shape[1])
        whose = lax.broadcasted_iota(jnp.int32, shape, 0)
        block = lax.broadcasted_iota(jnp.int32, shape, 1)
        spot = jnp.broadcast_to(rows_to[...] * NBL + cols_to[...], shape)
        match = jnp.broadcast_to(owner[...], shape) == whose
        first = jnp.min(jnp.where(match, block, shape[1]), axis=1, keepdims=True)
        second = jnp.max(jnp.where(match, block, -1), axis=1, keepdims=True)
        nowhere = front.shape[0] * 16 * CAP
        square = (128, BLK)
        for j, (chosen, there) in enumerate(
            ((first, second >= 0), (second, second > first))
        ):
            hit = jnp.max(jnp.where(block == chosen, spot, 0), axis=1, keepdims=True)
            hit = jnp.where(there, hit, nowhere)
            places[pl.ds(j, 128, stride=CAP), :] = jnp.broadcast_to(hit, square)
            index = jnp.broadcast_to(jnp.where(there, chosen, 0), square)
            diagonal = lax.broadcasted_iota(jnp.int32, square, 0) == lax.broadcasted_iota(
                jnp.int32, square, 1
            )
            chain_v[j : j + 1, :] = jnp.sum(
                jnp.where(diagonal, index, 0), axis=0, keepdims=True
            )
        copy = pltpu.make_async_copy(chain_v, chain, chain_sem)
        copy.start()

        def spread(d, carry):
            m0[d // 16, (d // 4) % 4, d % 4] = places[pl.ds(d * CAP, CAP), :]
            return carry

        lax.fori_loop(0, 128, spread, 0)
        copy.wait()

    def fill(d, carry):
        for j in range(CAP):
            slots[d // 16, (d // 4) % 4, d % 4, pl.ds(j * BLK, BLK), :] = blocks_v[chain[j, d]]
        return carry

    chains = []
    for part, (rows, order) in enumerate(zip(PARTS, ORDERS)):
        chains.append(((slots, rows), (stage1, rows), (out, rows), (arrived, rows), order))
    chains.append(((m0, None), (m1, None), (m2, None), (m3, None), (0, 1, 2)))

    def view(buffer, axis, where):
        ref, rows = buffer
        return ref.at[at_axis(axis, where, rows)]

    pending = {}

    def start(part, stage):
        steps = chains[part]
        source, target, axis = steps[stage], steps[stage + 1], steps[4][stage]
        own = pltpu.make_async_copy(
            view(source, axis, me[axis]), view(target, axis, me[axis]), own_sem.at[part, stage]
        )
        own.start()
        for d in offsets[axis]:
            there = peer(axis, d)
            pltpu.make_async_remote_copy(
                src_ref=view(source, axis, there),
                dst_ref=view(target, axis, me[axis]),
                send_sem=send_sem.at[part, stage],
                recv_sem=recv_sem.at[part, stage],
                device_id=device(axis, there),
                device_id_type=MESH,
            ).start()
        count = len(offsets[axis])
        whole = pltpu.make_async_remote_copy(
            src_ref=view(source, axis, pl.ds(0, count)),
            dst_ref=view(target, axis, pl.ds(0, count)),
            send_sem=send_sem.at[part, stage],
            recv_sem=recv_sem.at[part, stage],
            device_id=device(axis, peer(axis, 1)),
            device_id_type=MESH,
        )
        pending[part, stage] = (own, whole)

    def finish(part, stage):
        own, whole = pending[part, stage]
        own.wait()
        whole.wait_recv()

    gathers = []
    got = {}

    def place(half, dp, ds):
        if half == 0:
            return (y + dp + 4) % 4, (z + ds + 4) % 4
        return (y + ds + 4) % 4, (z + dp + 4) % 4

    def give(key, half, dp, ds, piece, along, step):
        py, pz = place(half, dp, ds)
        first, count = half * 256, 256
        if piece is not None:
            first, count = first + 128 * piece, 128
        rows = pl.ds(first, count)
        axis = (1, 2)[half] if along == 0 else (2, 1)[half]
        source = panel.at[rows] if (dp, ds) == (0, 0) else panel_full.at[py, pz, rows]
        index = len(gathers)
        copy = pltpu.make_async_remote_copy(
            src_ref=source,
            dst_ref=panel_full.at[py, pz, rows],
            send_sem=gsend_sem.at[index],
            recv_sem=grecv_sem.at[index],
            device_id=device(axis, peer(axis, step % 4)),
            device_id_type=MESH,
        )
        copy.start()
        gathers.append(copy)
        got[key] = copy

    def each(act):
        for half in (0, 1):
            for step, piece in ((1, 0), (-1, 1)):
                act(half, step, piece)

    def first_line():
        each(lambda h, s, p: give((h, "p", s), h, 0, 0, None, 0, s))

    def second_line(dp):
        each(lambda h, s, p: give((h, "s", dp, s), h, dp, 0, None, 1, s))

    def first_forward():
        each(lambda h, s, p: got[h, "p", s].wait_recv())
        each(lambda h, s, p: give((h, "pf", s), h, -s, 0, p, 0, s))

    def second_forward(dp):
        each(lambda h, s, p: got[h, "s", dp, s].wait_recv())
        each(lambda h, s, p: give((h, "sf", dp, s), h, dp, -s, p, 1, s))

    def landed(kind, *rest):
        each(lambda h, s, p: got[(h, kind) + rest + (s,)].wait_recv())

    def make_tables():
        def spread(d, carry):
            places[pl.ds(d * CAP, CAP), :] = m3[d // 16, (d // 4) % 4, d % 4]
            return carry

        lax.fori_loop(0, 128, spread, 0)
        where = places[...]
        slot = lax.broadcasted_iota(jnp.int32, where.shape, 0)
        lane = lax.broadcasted_iota(jnp.int32, where.shape, 1)

        def latest(same):
            found = jnp.max(jnp.where(same, slot, -1), axis=0, keepdims=True)
            return jnp.where(found < 0, CAP * 128, found)

        for half in range(2):
            mine = lane + half * BLK
            along = jnp.sum(jnp.where(slot == mine, where, 0), axis=0, keepdims=True)
            same = jnp.logical_and(where == along, slot < mine)
            chain_v[half : half + 1, :] = latest(same)
        for third in range(3):
            same = where == lane + third * BLK
            chain_v[2 + third : 3 + third, :] = latest(same)
        copy = pltpu.make_async_copy(chain_v, chain, chain_sem)
        copy.start()
        copy.wait()

    def block_of(t):
        d = t // CAP
        return slots[d // 16, (d // 4) % 4, d % 4, pl.ds((t % CAP) * BLK, BLK), :].astype(
            jnp.float32
        )

    count = sums.shape[0] - 1

    def add_up(arrivals):
        sums[count] = jnp.zeros((BLK, BLK), jnp.float32)

        def one(t, carry):
            sums[t] = block_of(t) + sums[chain[t // BLK, t % BLK]]
            return carry

        each_time = count // len(arrivals)
        for i, copy in enumerate(arrivals):
            copy.wait()
            lax.fori_loop(i * each_time, (i + 1) * each_time, one, 0)

    def assembled(source, row):
        d = 2 * row % 16
        for i, wide in enumerate((wide0, wide1)):
            wide[pl.ds(0, 256), :] = source[d // 4, d % 4 + i].astype(jnp.float32)
        values = []
        for k in range(NBL):
            p = row * NBL + k
            total = sums[chain[2 + p // BLK, p % BLK]]
            part = pl.ds(k, BLK // 2, stride=NBL)
            value = jnp.concatenate([wide0[part, :], wide1[part, :]], axis=0)
            values.append((value + total).astype(jnp.bfloat16))
        return d, values

    def make_factor():
        def one(row, carry):
            _, values = assembled(stage1.at[0], row)
            for k in range(NBL):
                top[pl.ds(row * BLK, BLK), pl.ds(k * BLK, BLK)] = values[k]
            return carry

        lax.fori_loop(0, PIV // BLK, one, 0)
        load_pivot.wait()
        factor[...] = jnp.dot(
            pivot_v[...], top[...], preferred_element_type=jnp.float32
        ).astype(jnp.bfloat16)

    def make_lower():
        for i in range(8):
            load_lower[i].wait()

            def one(j, carry):
                d, values = assembled(slots.at[i], PIV // BLK + i * 8 + j)
                for k in range(NBL):
                    slots[i, d // 4, d % 4 + k // 2, pl.ds(k % 2 * BLK, BLK), :] = values[k]
                return carry

            lax.fori_loop(0, 8, one, 0)

    limit = size[0]

    def load(i, half, decode):
        rows = pl.ds(half * 256, 256)
        if decode is None:
            source = panel.at[rows]
        else:
            py, pz = decode(i, half)
            source = panel_full.at[py, pz, rows]
        return pltpu.make_async_copy(
            source, panel_v.at[i % DEPTH, half], panel_sem.at[i % DEPTH, half]
        )

    def prefetch(first, count, decode):
        for i in range(min(DEPTH, count)):
            for half in (0, 1):
                load(first + i, half, None if first + i == 0 else decode).start()

    def updates(first, count, decode):
        def lower(row, k):
            d = 2 * row
            return slots[d // 16, (d // 4) % 4, d % 4 + k // 2, pl.ds(k % 2 * BLK, BLK), :]

        def write(d, value):
            out[d // 16, (d // 4) % 4, d % 4] = value

        def one(i, carry):
            for half, update in ((0, update0), (1, update1)):
                load(i, half, decode).wait()
                update[...] = jnp.dot(
                    panel_v[i % DEPTH, half], factor[...], preferred_element_type=jnp.float32
                )
            for half, update in ((0, update0), (1, update1)):
                py, pz = decode(i, half)
                first_row = (py * 4 + pz) * 4 + half * 2
                schur_rows(update, (wide0, wide1), lower, write, pattern, limit, g, first_row)

            if count > DEPTH:

                @pl.when(i + DEPTH < first + count)
                def _():
                    for half in (0, 1):
                        load(i + DEPTH, half, decode).start()

            return carry

        lax.fori_loop(first, first + count, one, 0)

    def spot(half, dp, ds):
        return (y + dp * (1 - half) + ds * half) % 4, (z + dp * half + ds * (1 - half)) % 4

    def near(i, half):
        a, b = i % 3, i // 3
        return spot(half, a + a // 2, b + b // 2)

    def middle(i, half):
        return spot(half, 2 * (1 - (i - 9) // 3), (i - 6) % 4)

    def late(i, half):
        return spot(half, 3 - 2 * (i - 13), 2)

    pl.semaphore_wait(barrier, 13)
    first_line()
    load_pivot.start()
    make_slots()
    start(3, 0)
    load_blocks.wait()
    lax.fori_loop(0, 128, fill, 0)
    for part in range(3):
        start(part, 0)
    second_line(0)
    finish(3, 0)
    start(3, 1)
    for part in range(3):
        finish(part, 0)
        start(part, 1)
    finish(3, 1)
    start(3, 2)
    first_forward()
    second_forward(0)
    for part in range(3):
        finish(part, 1)
        start(part, 2)
    second_line(-1)
    finish(3, 2)
    make_tables()
    for part in range(3):
        pending[part, 0][1].wait_send()
        pending[part, 1][1].wait_send()
    load_top.start()
    for part in range(3):
        finish(part, 2)
    back = [
        pltpu.make_async_copy(arrived.at[i], slots.at[i], arrived_sem.at[i]) for i in range(8)
    ]
    for copy in back:
        copy.start()
    second_line(1)
    landed("pf")
    second_line(2)
    second_forward(-1)
    add_up(back)
    for copy in load_lower:
        copy.start()
    second_forward(1)
    prefetch(0, 9, near)
    load_top.wait()
    make_factor()
    make_lower()
    for part in range(3):
        pending[part, 2][1].wait_send()
    final = (y + 2) % 4 * 4 + (z + 2) % 4
    leave_rows = pltpu.make_async_copy(
        slots.at[final // 2, pl.ds(final % 2 * 2, 2)],
        out.at[final // 2, pl.ds(final % 2 * 2, 2)],
        leave_sem,
    )
    leave_rows.start()
    updates(0, 9, near)
    second_forward(2)
    landed("sf", 0)
    prefetch(9, 4, middle)
    updates(9, 4, middle)
    for i, dp in ((13, -1), (14, 1)):
        landed("sf", dp)
        prefetch(i, 1, late)
        updates(i, 1, late)
    leave_rows.wait()
    landed("sf", 2)
    for (part, stage), (_, whole) in pending.items():
        if part == 3:
            whole.wait_send()
    for copy in gathers:
        copy.wait_send()


def front_parts(size, pattern, owner, rows_to, cols_to, blocks, front, pivot, panel):
    grid_of = (8, 4, 4)
    any_space = pl.BlockSpec(memory_space=pl.ANY)
    smem = pl.BlockSpec(memory_space=pltpu.SMEM)
    vmem = pl.BlockSpec(memory_space=pltpu.VMEM)
    dma = pltpu.SemaphoreType.DMA
    outs = [
        pltpu.VMEM(grid_of + (CAP * BLK, BLK), jnp.bfloat16),
        jax.ShapeDtypeStruct(grid_of + (CAP * BLK, BLK), jnp.bfloat16),
        jax.ShapeDtypeStruct((4, 4) + panel.shape, jnp.bfloat16),
        pltpu.VMEM((PIV, NBL * BLK), jnp.bfloat16),
    ]
    small = pltpu.VMEM(grid_of + (CAP, BLK), jnp.int32)
    large = pltpu.VMEM(grid_of + (CAP * BLK, BLK), jnp.bfloat16)
    return pl.pallas_call(
        front_kernel,
        out_shape=outs,
        in_specs=[smem, smem, vmem, vmem, vmem] + [any_space] * 4,
        out_specs=[vmem, any_space, any_space, vmem],
        scratch_shapes=[
            large, large,
            pltpu.VMEM(blocks.shape, jnp.bfloat16),
            pltpu.VMEM((128 * CAP + 1, BLK, BLK), jnp.float32),
            pltpu.VMEM(pivot.shape, jnp.bfloat16),
            pltpu.VMEM((PIV, NBL * BLK), jnp.bfloat16),
            pltpu.VMEM((DEPTH, 2, 256, PIV), jnp.bfloat16),
            pltpu.VMEM((256, NBL * BLK), jnp.float32),
            pltpu.VMEM((256, NBL * BLK), jnp.float32),
            pltpu.VMEM((BLK * NBL, BLK), jnp.float32),
            pltpu.VMEM((BLK * NBL, BLK), jnp.float32),
            small, small, small, small,
            pltpu.VMEM((128 * CAP, BLK), jnp.int32),
            pltpu.VMEM((8, BLK), jnp.int32),
            pltpu.SMEM((8, BLK), jnp.int32),
            dma((4, 3)), dma((4, 3)), dma((4, 3)),
            dma((40,)), dma((40,)),
            dma((3,)), dma((8,)), dma((8,)), dma, dma((DEPTH, 2)), dma,
        ],
        compiler_params=pltpu.CompilerParams(
            collective_id=0, has_side_effects=True, vmem_limit_bytes=50 * 2**20
        ),
        name="front",
    )(size, pattern, owner, rows_to, cols_to, blocks, front, pivot, panel)


def last_kernel(
    size, pattern, parts, panel_full, factor, out,
    factor_v, panel_v, lower_v, update0, update1, result, wide0, wide1,
    load_sem, part_sem, out_sem,
):
    g = lax.axis_index("grid")
    final = (g // 4 + 2) % 4 * 4 + (g % 4 + 2) % 4
    loads = [
        pltpu.make_async_copy(factor, factor_v, load_sem.at[0]),
        pltpu.make_async_copy(panel_full.at[final // 4, final % 4], panel_v, load_sem.at[1]),
        pltpu.make_async_copy(parts.at[pl.ds(final * 8, 8)], lower_v, load_sem.at[2]),
    ]
    for copy in loads:
        copy.start()
    passed = []
    for i in range(1, 16):
        rows = pl.ds((final + i) % 16 * 8, 8)
        passed.append(pltpu.make_async_copy(parts.at[rows], out.at[rows], part_sem.at[i - 1]))
        passed[-1].start()
    for copy in loads:
        copy.wait()

    def lower(row, k):
        return lower_v[2 * (row - final * 4) + k // 2, pl.ds(k % 2 * BLK, BLK), :]

    def write(d, value):
        result[d - final * 8] = value

    for half, update in ((0, update0), (1, update1)):
        update[...] = jnp.dot(
            panel_v[pl.ds(half * 256, 256)], factor_v[...], preferred_element_type=jnp.float32
        )
    for half, update in ((0, update0), (1, update1)):
        first_row = final * 4 + half * 2
        schur_rows(update, (wide0, wide1), lower, write, pattern, size[0], g, first_row)
        done = pltpu.make_async_copy(
            result.at[pl.ds(half * 4, 4)],
            out.at[pl.ds(final * 8 + half * 4, 4)],
            out_sem.at[half],
        )
        done.start()
        passed.append(done)
    for copy in passed:
        copy.wait()


def last_part(size, pattern, parts, panel_full, factor):
    any_space = pl.BlockSpec(memory_space=pl.ANY)
    smem = pl.BlockSpec(memory_space=pltpu.SMEM)
    half = pltpu.VMEM((256, NBL * BLK), jnp.float32)
    wide = pltpu.VMEM((BLK * NBL, BLK), jnp.float32)
    rows = pltpu.VMEM((8, CAP * BLK, BLK), jnp.bfloat16)
    dma = pltpu.SemaphoreType.DMA
    return pl.pallas_call(
        last_kernel,
        out_shape=jax.ShapeDtypeStruct(parts.shape, parts.dtype),
        in_specs=[smem, smem] + [any_space] * 3,
        out_specs=any_space,
        scratch_shapes=[
            pltpu.VMEM(factor.shape, jnp.bfloat16),
            pltpu.VMEM(panel_full.shape[2:], jnp.bfloat16),
            rows, half, half, rows, wide, wide,
            dma((3,)), dma((15,)), dma((2,)),
        ],
        compiler_params=pltpu.CompilerParams(vmem_limit_bytes=36 * 2**20),
        name="last_part",
    )(size, pattern, parts, panel_full, factor)


def per_device(
    front_entries,
    contributions,
    dest_owner,
    dest_row,
    dest_col,
    pivot_inverse,
    panel,
    pattern,
    front_size,
):
    pattern = pattern[0, :, :, 0].T.reshape(NBL, 1, -1)
    parts, _, panel_full, factor = front_parts(
        front_size,
        pattern,
        dest_owner.reshape(1, -1),
        dest_row.reshape(1, -1),
        dest_col.reshape(1, -1),
        contributions,
        front_entries.reshape(-1, 4, 4, CAP * BLK, BLK),
        pivot_inverse[0],
        panel[0],
    )
    parts = parts.reshape(-1, CAP * BLK, BLK)
    out = last_part(front_size, pattern, parts, panel_full, factor)
    return out.reshape(1, -1, NBL, BLK)


def solution(mesh):
    placed = (
        P("front", None, None, "grid"),
        P(("front", "grid"), None, None),
        P(("front", "grid"), None),
        P(("front", "grid")),
        P(("front", "grid")),
        P("front", None, None),
        P("front", "grid", None),
        P("front", None, None, "grid"),
        P("front"),
    )
    return jax.shard_map(
        per_device,
        mesh=mesh,
        in_specs=placed,
        out_specs=P("front", None, None, "grid"),
        check_vma=False,
    )
```

```python
import functools

import jax
import jax.numpy as jnp
from jax import lax
from jax.experimental import pallas as pl
from jax.experimental.pallas import tpu as pltpu
from jax.sharding import PartitionSpec as P

BLK = 128
PIV = 1024
NBL = 4
CAP = 2
MESH = pl.DeviceIdType.MESH
PARTS = ((0, 96), (96, 80), (176, 80))
DEPTH = 4
ORDERS = ((0, 1, 2), (1, 2, 0), (2, 0, 1))


def at_axis(axis, where, rows=None):
    index = [slice(None)] * 5
    index[axis] = where
    if rows is not None:
        index[3] = pl.ds(rows[0], rows[1])
    return tuple(index)


def schur_rows(update, wides, lower, write, pattern, limit, column, first):
    for j, wide in enumerate(wides):
        row = first + j
        for k in range(NBL):
            keep = jnp.logical_and(row < limit, k * 16 + column < limit)
            chosen = pattern[k, 0, row].astype(jnp.float32)
            taken = update[pl.ds(j * BLK, BLK), pl.ds(k * BLK, BLK)]
            here = lower(row, k).astype(jnp.float32)
            wide[pl.ds(k, BLK, stride=NBL), :] = jnp.where(keep, here - chosen * taken, 0.0)
        for part in range(2):
            write(row * 2 + part, wide[pl.ds(part * 256, 256), :].astype(jnp.bfloat16))


def front_kernel(
    size, pattern, owner, rows_to, cols_to, blocks, front, pivot, panel,
    out, arrived, panel_full, factor,
    slots, stage1, blocks_v, sums, pivot_v, top, panel_v,
    update0, update1, wide0, wide1,
    m0, m1, m2, m3, places, chain_v, chain,
    send_sem, recv_sem, own_sem, gsend_sem, grecv_sem,
    load_sem, lower_sem, arrived_sem, chain_sem, panel_sem, leave_sem,
):
    f = lax.axis_index("front")
    g = lax.axis_index("grid")
    y, z = g // 4, g % 4
    me = (f, y, z)

    def device(axis, coordinate):
        if axis == 0:
            return (coordinate, g)
        if axis == 1:
            return (f, coordinate * 4 + z)
        return (f, y * 4 + coordinate)

    def peer(axis, d):
        if axis == 0:
            return ((f // 2 + d // 2) % 4) * 2 + (f + d) % 2
        return (me[axis] + d) % 4

    offsets = ((4, 5, 2, 6, 3, 7, 1), (2, 1, 3), (2, 1, 3))

    barrier = pltpu.get_barrier_semaphore()
    for axis in range(3):
        for d in offsets[axis]:
            pl.semaphore_signal(
                barrier, inc=1, device_id=device(axis, peer(axis, d)), device_id_type=MESH
            )

    load_blocks = pltpu.make_async_copy(blocks, blocks_v, load_sem.at[0])
    load_top = pltpu.make_async_copy(front.at[0], stage1.at[0], load_sem.at[1])
    load_pivot = pltpu.make_async_copy(pivot, pivot_v, load_sem.at[2])
    load_lower = [
        pltpu.make_async_copy(front.at[1 + i], slots.at[i], lower_sem.at[i]) for i in range(8)
    ]
    load_blocks.start()

    def make_slots():
        shape = (128, owner.shape[1])
        whose = lax.broadcasted_iota(jnp.int32, shape, 0)
        block = lax.broadcasted_iota(jnp.int32, shape, 1)
        spot = jnp.broadcast_to(rows_to[...] * NBL + cols_to[...], shape)
        match = jnp.broadcast_to(owner[...], shape) == whose
        first = jnp.min(jnp.where(match, block, shape[1]), axis=1, keepdims=True)
        second = jnp.max(jnp.where(match, block, -1), axis=1, keepdims=True)
        nowhere = front.shape[0] * 16 * CAP
        square = (128, BLK)
        lane = lax.broadcasted_iota(jnp.int32, square, 1)
        hits = []
        for j, (chosen, there) in enumerate(
            ((first, second >= 0), (second, second > first))
        ):
            hit = jnp.max(jnp.where(block == chosen, spot, 0), axis=1, keepdims=True)
            hit = jnp.where(there, hit, nowhere)
            hits.append(jnp.broadcast_to(hit, square))
            index = jnp.broadcast_to(jnp.where(there, chosen, 0), square)
            diagonal = lax.broadcasted_iota(jnp.int32, square, 0) == lane
            chain_v[j : j + 1, :] = jnp.sum(
                jnp.where(diagonal, index, 0), axis=0, keepdims=True
            )
        copy = pltpu.make_async_copy(chain_v, chain, chain_sem)
        copy.start()
        places[pl.ds(0, 128), :] = jnp.where(lane < BLK // CAP, *hits)

        def spread(d, carry):
            m0[d // 16, (d // 4) % 4, d % 4] = places[pl.ds(d, 1), :]
            return carry

        lax.fori_loop(0, 128, spread, 0)
        copy.wait()

    def fill(d, carry):
        for j in range(CAP):
            slots[d // 16, (d // 4) % 4, d % 4, pl.ds(j * BLK, BLK), :] = blocks_v[chain[j, d]]
        return carry

    chains = []
    for part, (rows, order) in enumerate(zip(PARTS, ORDERS)):
        chains.append(((slots, rows), (stage1, rows), (out, rows), (arrived, rows), order))
    chains.append(((m0, None), (m1, None), (m2, None), (m3, None), (0, 1, 2)))

    def view(buffer, axis, where):
        ref, rows = buffer
        return ref.at[at_axis(axis, where, rows)]

    pending = {}

    def start(part, stage):
        steps = chains[part]
        source, target, axis = steps[stage], steps[stage + 1], steps[4][stage]
        own = pltpu.make_async_copy(
            view(source, axis, me[axis]), view(target, axis, me[axis]), own_sem.at[part, stage]
        )
        own.start()
        for d in offsets[axis]:
            there = peer(axis, d)
            pltpu.make_async_remote_copy(
                src_ref=view(source, axis, there),
                dst_ref=view(target, axis, me[axis]),
                send_sem=send_sem.at[part, stage],
                recv_sem=recv_sem.at[part, stage],
                device_id=device(axis, there),
                device_id_type=MESH,
            ).start()
        count = len(offsets[axis])
        whole = pltpu.make_async_remote_copy(
            src_ref=view(source, axis, pl.ds(0, count)),
            dst_ref=view(target, axis, pl.ds(0, count)),
            send_sem=send_sem.at[part, stage],
            recv_sem=recv_sem.at[part, stage],
            device_id=device(axis, peer(axis, 1)),
            device_id_type=MESH,
        )
        pending[part, stage] = (own, whole)

    def finish(part, stage):
        own, whole = pending[part, stage]
        own.wait()
        whole.wait_recv()

    gathers = []
    got = {}

    def place(half, dp, ds):
        if half == 0:
            return (y + dp + 4) % 4, (z + ds + 4) % 4
        return (y + ds + 4) % 4, (z + dp + 4) % 4

    def give(key, half, dp, ds, piece, along, step):
        py, pz = place(half, dp, ds)
        first, count = half * 256, 256
        if piece is not None:
            first, count = first + 128 * piece, 128
        rows = pl.ds(first, count)
        axis = (1, 2)[half] if along == 0 else (2, 1)[half]
        source = panel.at[rows] if (dp, ds) == (0, 0) else panel_full.at[py, pz, rows]
        index = len(gathers)
        copy = pltpu.make_async_remote_copy(
            src_ref=source,
            dst_ref=panel_full.at[py, pz, rows],
            send_sem=gsend_sem.at[index],
            recv_sem=grecv_sem.at[index],
            device_id=device(axis, peer(axis, step % 4)),
            device_id_type=MESH,
        )
        copy.start()
        gathers.append(copy)
        got[key] = copy

    def each(act):
        for half in (0, 1):
            for step, piece in ((1, 0), (-1, 1)):
                act(half, step, piece)

    def first_line():
        each(lambda h, s, p: give((h, "p", s), h, 0, 0, None, 0, s))

    def second_line(dp):
        each(lambda h, s, p: give((h, "s", dp, s), h, dp, 0, None, 1, s))

    def first_forward():
        each(lambda h, s, p: got[h, "p", s].wait_recv())
        each(lambda h, s, p: give((h, "pf", s), h, -s, 0, p, 0, s))

    def second_forward(dp):
        each(lambda h, s, p: got[h, "s", dp, s].wait_recv())
        each(lambda h, s, p: give((h, "sf", dp, s), h, dp, -s, p, 1, s))

    def landed(kind, *rest):
        each(lambda h, s, p: got[(h, kind) + rest + (s,)].wait_recv())

    def make_tables():
        def spread(d, carry):
            places[pl.ds(d, 1), :] = m3[d // 16, (d // 4) % 4, d % 4]
            return carry

        lax.fori_loop(0, 128, spread, 0)
        both = places[pl.ds(0, 128), :]
        part = lax.broadcasted_iota(jnp.int32, both.shape, 1) // (BLK // CAP)
        for j in range(CAP):
            mine = jnp.max(jnp.where(part == j, both, 0), axis=1, keepdims=True)
            places[pl.ds(j, 128, stride=CAP), :] = jnp.broadcast_to(mine, both.shape)
        where = places[...]
        slot = lax.broadcasted_iota(jnp.int32, where.shape, 0)
        lane = lax.broadcasted_iota(jnp.int32, where.shape, 1)

        def latest(same):
            found = jnp.max(jnp.where(same, slot, -1), axis=0, keepdims=True)
            return jnp.where(found < 0, CAP * 128, found)

        for half in range(2):
            mine = lane + half * BLK
            along = jnp.sum(jnp.where(slot == mine, where, 0), axis=0, keepdims=True)
            same = jnp.logical_and(where == along, slot < mine)
            chain_v[half : half + 1, :] = latest(same)
        for third in range(3):
            same = where == lane + third * BLK
            chain_v[2 + third : 3 + third, :] = latest(same)
        copy = pltpu.make_async_copy(chain_v, chain, chain_sem)
        copy.start()
        copy.wait()

    def block_of(t):
        d = t // CAP
        return slots[d // 16, (d // 4) % 4, d % 4, pl.ds((t % CAP) * BLK, BLK), :].astype(
            jnp.float32
        )

    count = sums.shape[0] - 1

    def add_up(arrivals):
        sums[count] = jnp.zeros((BLK, BLK), jnp.float32)

        def one(t, carry):
            sums[t] = block_of(t) + sums[chain[t // BLK, t % BLK]]
            return carry

        each_time = count // len(arrivals)
        for i, copy in enumerate(arrivals):
            copy.wait()
            lax.fori_loop(i * each_time, (i + 1) * each_time, one, 0)

    def assembled(source, row):
        d = 2 * row % 16
        for i, wide in enumerate((wide0, wide1)):
            wide[pl.ds(0, 256), :] = source[d // 4, d % 4 + i].astype(jnp.float32)
        values = []
        for k in range(NBL):
            p = row * NBL + k
            total = sums[chain[2 + p // BLK, p % BLK]]
            part = pl.ds(k, BLK // 2, stride=NBL)
            value = jnp.concatenate([wide0[part, :], wide1[part, :]], axis=0)
            values.append((value + total).astype(jnp.bfloat16))
        return d, values

    def make_factor():
        def one(row, carry):
            _, values = assembled(stage1.at[0], row)
            for k in range(NBL):
                top[pl.ds(row * BLK, BLK), pl.ds(k * BLK, BLK)] = values[k]
            return carry

        lax.fori_loop(0, PIV // BLK, one, 0)
        load_pivot.wait()
        factor[...] = jnp.dot(
            pivot_v[...], top[...], preferred_element_type=jnp.float32
        ).astype(jnp.bfloat16)

    def make_lower():
        for i in range(8):
            load_lower[i].wait()

            def one(j, carry):
                d, values = assembled(slots.at[i], PIV // BLK + i * 8 + j)
                for k in range(NBL):
                    slots[i, d // 4, d % 4 + k // 2, pl.ds(k % 2 * BLK, BLK), :] = values[k]
                return carry

            lax.fori_loop(0, 8, one, 0)

    limit = size[0]

    def load(i, half, decode):
        rows = pl.ds(half * 256, 256)
        if decode is None:
            source = panel.at[rows]
        else:
            py, pz = decode(i, half)
            source = panel_full.at[py, pz, rows]
        return pltpu.make_async_copy(
            source, panel_v.at[i % DEPTH, half], panel_sem.at[i % DEPTH, half]
        )

    def prefetch(first, count, decode):
        for i in range(min(DEPTH, count)):
            for half in (0, 1):
                load(first + i, half, None if first + i == 0 else decode).start()

    def updates(first, count, decode):
        def lower(row, k):
            d = 2 * row
            return slots[d // 16, (d // 4) % 4, d % 4 + k // 2, pl.ds(k % 2 * BLK, BLK), :]

        def write(d, value):
            out[d // 16, (d // 4) % 4, d % 4] = value

        def one(i, carry):
            for half, update in ((0, update0), (1, update1)):
                load(i, half, decode).wait()
                update[...] = jnp.dot(
                    panel_v[i % DEPTH, half], factor[...], preferred_element_type=jnp.float32
                )
            for half, update in ((0, update0), (1, update1)):
                py, pz = decode(i, half)
                first_row = (py * 4 + pz) * 4 + half * 2
                schur_rows(update, (wide0, wide1), lower, write, pattern, limit, g, first_row)

            if count > DEPTH:

                @pl.when(i + DEPTH < first + count)
                def _():
                    for half in (0, 1):
                        load(i + DEPTH, half, decode).start()

            return carry

        lax.fori_loop(first, first + count, one, 0)

    def spot(half, dp, ds):
        return (y + dp * (1 - half) + ds * half) % 4, (z + dp * half + ds * (1 - half)) % 4

    def near(i, half):
        a, b = i % 3, i // 3
        return spot(half, a + a // 2, b + b // 2)

    def middle(i, half):
        return spot(half, 2 * (1 - (i - 9) // 3), (i - 6) % 4)

    def late(i, half):
        return spot(half, 3 - 2 * (i - 13), 2)

    pl.semaphore_wait(barrier, 13)
    first_line()
    load_pivot.start()
    make_slots()
    start(3, 0)
    load_blocks.wait()
    lax.fori_loop(0, 128, fill, 0)
    for part in range(3):
        start(part, 0)
    second_line(0)
    finish(3, 0)
    start(3, 1)
    for part in range(3):
        finish(part, 0)
        start(part, 1)
    finish(3, 1)
    start(3, 2)
    first_forward()
    second_forward(0)
    for part in range(3):
        finish(part, 1)
        start(part, 2)
    second_line(-1)
    finish(3, 2)
    make_tables()
    for part in range(3):
        pending[part, 0][1].wait_send()
        pending[part, 1][1].wait_send()
    load_top.start()
    for part in range(3):
        finish(part, 2)
    back = [
        pltpu.make_async_copy(arrived.at[i], slots.at[i], arrived_sem.at[i]) for i in range(8)
    ]
    for copy in back:
        copy.start()
    second_line(1)
    landed("pf")
    second_line(2)
    second_forward(-1)
    add_up(back)
    for copy in load_lower:
        copy.start()
    second_forward(1)
    prefetch(0, 9, near)
    load_top.wait()
    make_factor()
    make_lower()
    for part in range(3):
        pending[part, 2][1].wait_send()
    final = (y + 2) % 4 * 4 + (z + 2) % 4
    leave_rows = pltpu.make_async_copy(
        slots.at[final // 2, pl.ds(final % 2 * 2, 2)],
        out.at[final // 2, pl.ds(final % 2 * 2, 2)],
        leave_sem,
    )
    leave_rows.start()
    updates(0, 9, near)
    second_forward(2)
    landed("sf", 0)
    prefetch(9, 4, middle)
    updates(9, 4, middle)
    for i, dp in ((13, -1), (14, 1)):
        landed("sf", dp)
        prefetch(i, 1, late)
        updates(i, 1, late)
    leave_rows.wait()
    landed("sf", 2)
    for (part, stage), (_, whole) in pending.items():
        if part == 3:
            whole.wait_send()
    for copy in gathers:
        copy.wait_send()


def front_parts(size, pattern, owner, rows_to, cols_to, blocks, front, pivot, panel):
    grid_of = (8, 4, 4)
    any_space = pl.BlockSpec(memory_space=pl.ANY)
    smem = pl.BlockSpec(memory_space=pltpu.SMEM)
    vmem = pl.BlockSpec(memory_space=pltpu.VMEM)
    dma = pltpu.SemaphoreType.DMA
    outs = [
        pltpu.VMEM(grid_of + (CAP * BLK, BLK), jnp.bfloat16),
        jax.ShapeDtypeStruct(grid_of + (CAP * BLK, BLK), jnp.bfloat16),
        jax.ShapeDtypeStruct((4, 4) + panel.shape, jnp.bfloat16),
        pltpu.VMEM((PIV, NBL * BLK), jnp.bfloat16),
    ]
    small = pltpu.VMEM(grid_of + (1, BLK), jnp.int32)
    large = pltpu.VMEM(grid_of + (CAP * BLK, BLK), jnp.bfloat16)
    return pl.pallas_call(
        front_kernel,
        out_shape=outs,
        in_specs=[smem, smem, vmem, vmem, vmem] + [any_space] * 4,
        out_specs=[vmem, any_space, any_space, vmem],
        scratch_shapes=[
            large, large,
            pltpu.VMEM(blocks.shape, jnp.bfloat16),
            pltpu.VMEM((128 * CAP + 1, BLK, BLK), jnp.float32),
            pltpu.VMEM(pivot.shape, jnp.bfloat16),
            pltpu.VMEM((PIV, NBL * BLK), jnp.bfloat16),
            pltpu.VMEM((DEPTH, 2, 256, PIV), jnp.bfloat16),
            pltpu.VMEM((256, NBL * BLK), jnp.float32),
            pltpu.VMEM((256, NBL * BLK), jnp.float32),
            pltpu.VMEM((BLK * NBL, BLK), jnp.float32),
            pltpu.VMEM((BLK * NBL, BLK), jnp.float32),
            small, small, small, small,
            pltpu.VMEM((128 * CAP, BLK), jnp.int32),
            pltpu.VMEM((8, BLK), jnp.int32),
            pltpu.SMEM((8, BLK), jnp.int32),
            dma((4, 3)), dma((4, 3)), dma((4, 3)),
            dma((40,)), dma((40,)),
            dma((3,)), dma((8,)), dma((8,)), dma, dma((DEPTH, 2)), dma,
        ],
        compiler_params=pltpu.CompilerParams(
            collective_id=0, has_side_effects=True, vmem_limit_bytes=50 * 2**20
        ),
        name="front",
    )(size, pattern, owner, rows_to, cols_to, blocks, front, pivot, panel)


def last_kernel(
    size, pattern, parts, panel_full, factor, out,
    factor_v, panel_v, lower_v, update0, update1, result, wide0, wide1,
    load_sem, part_sem, out_sem,
):
    g = lax.axis_index("grid")
    final = (g // 4 + 2) % 4 * 4 + (g % 4 + 2) % 4
    loads = [
        pltpu.make_async_copy(factor, factor_v, load_sem.at[0]),
        pltpu.make_async_copy(parts.at[pl.ds(final * 8, 8)], lower_v, load_sem.at[1]),
    ] + [
        pltpu.make_async_copy(
            panel_full.at[final // 4, final % 4, pl.ds(half * 256, 256)],
            panel_v.at[pl.ds(half * 256, 256)],
            load_sem.at[2 + half],
        )
        for half in (0, 1)
    ]
    for copy in loads:
        copy.start()
    passed = []
    for i in range(1, 16):
        rows = pl.ds((final + i) % 16 * 8, 8)
        passed.append(pltpu.make_async_copy(parts.at[rows], out.at[rows], part_sem.at[i - 1]))
        passed[-1].start()
    for copy in loads[:2]:
        copy.wait()

    def lower(row, k):
        return lower_v[2 * (row - final * 4) + k // 2, pl.ds(k % 2 * BLK, BLK), :]

    def write(d, value):
        result[d - final * 8] = value

    for half, update in ((0, update0), (1, update1)):
        loads[2 + half].wait()
        update[...] = jnp.dot(
            panel_v[pl.ds(half * 256, 256)], factor_v[...], preferred_element_type=jnp.float32
        )
        first_row = final * 4 + half * 2
        schur_rows(update, (wide0, wide1), lower, write, pattern, size[0], g, first_row)
        done = pltpu.make_async_copy(
            result.at[pl.ds(half * 4, 4)],
            out.at[pl.ds(final * 8 + half * 4, 4)],
            out_sem.at[half],
        )
        done.start()
        passed.append(done)
    for copy in passed:
        copy.wait()


def last_part(size, pattern, parts, panel_full, factor):
    any_space = pl.BlockSpec(memory_space=pl.ANY)
    smem = pl.BlockSpec(memory_space=pltpu.SMEM)
    half = pltpu.VMEM((256, NBL * BLK), jnp.float32)
    wide = pltpu.VMEM((BLK * NBL, BLK), jnp.float32)
    rows = pltpu.VMEM((8, CAP * BLK, BLK), jnp.bfloat16)
    dma = pltpu.SemaphoreType.DMA
    return pl.pallas_call(
        last_kernel,
        out_shape=jax.ShapeDtypeStruct(parts.shape, parts.dtype),
        in_specs=[smem, smem] + [any_space] * 3,
        out_specs=any_space,
        scratch_shapes=[
            pltpu.VMEM(factor.shape, jnp.bfloat16),
            pltpu.VMEM(panel_full.shape[2:], jnp.bfloat16),
            rows, half, half, rows, wide, wide,
            dma((4,)), dma((15,)), dma((2,)),
        ],
        compiler_params=pltpu.CompilerParams(vmem_limit_bytes=36 * 2**20),
        name="last_part",
    )(size, pattern, parts, panel_full, factor)


def per_device(
    front_entries,
    contributions,
    dest_owner,
    dest_row,
    dest_col,
    pivot_inverse,
    panel,
    pattern,
    front_size,
):
    pattern = pattern[0, :, :, 0].T.reshape(NBL, 1, -1)
    parts, _, panel_full, factor = front_parts(
        front_size,
        pattern,
        dest_owner.reshape(1, -1),
        dest_row.reshape(1, -1),
        dest_col.reshape(1, -1),
        contributions,
        front_entries.reshape(-1, 4, 4, CAP * BLK, BLK),
        pivot_inverse[0],
        panel[0],
    )
    parts = parts.reshape(-1, CAP * BLK, BLK)
    out = last_part(front_size, pattern, parts, panel_full, factor)
    return out.reshape(1, -1, NBL, BLK)


def solution(mesh):
    placed = (
        P("front", None, None, "grid"),
        P(("front", "grid"), None, None),
        P(("front", "grid"), None),
        P(("front", "grid")),
        P(("front", "grid")),
        P("front", None, None),
        P("front", "grid", None),
        P("front", None, None, "grid"),
        P("front"),
    )
    return jax.shard_map(
        per_device,
        mesh=mesh,
        in_specs=placed,
        out_specs=P("front", None, None, "grid"),
        check_vma=False,
    )
```
